256 devices in a mesh: blk: 64 (over z, y, core), col: 4 (over x).
Axes of the slice: x: 4, y: 4, z: 8, core: 2. Of those that a mesh axis runs over, the one named last changes fastest.
Arguments:
- y_start: float32 [128, 131072], P('col', 'blk')
- tile_real: bfloat16 [6144, 256, 256], P('blk'), may hold values from 0 to 1, as said below
- tile_imag: bfloat16 [6144, 256, 256], P('blk'), may hold values from -1 to 1, as said below
- tile_rows: int32 [6144], P('blk'), may hold values from 0 to 7
- tile_slots: int32 [6144], P('blk'), may hold values from 0 to 71, as said below
- fetch_pick: int32 [64, 64], P('blk'), may hold values from 0 to 7
Outputs:
- encodings: float32 [128, 131072], P('col', 'blk')
The draws below stay inside these ranges and needn't reach their ends.
Inputs may be any that keep to these rules, and one draw needn't show every extreme that they name: `tile_slots`: on each device the first 16 of its 96 tiles name an own row block (0 to 7); the others name 8 + p for an owning device p other than itself; every device reads from the devices 1, 32 and -1 places away along blk, modulo the axis. `tile_real`: entries are 0 or 1. `tile_imag`: entries are -1, 0 or 1, and never nonzero where tile_real is nonzero.
All inputs are finite; a program needn't handle non-finite values.
Results may differ from the reference program's by a relative error of at most 0.0031.
Values may be sent and summed in bfloat16 or wider, within the bound.
A program may use at most 128 MiB of HBM per device.

```python
import math
import jax
import jax.numpy as jnp
from jax import lax

B = 256
VEC2 = 128
RB_DEV = 8
LOC_RB = 2
REM_RB = 10
STEPS = 4
TILES_DEV = 96
TILES = 6144
BLOCKS = 512
NODES = 131072


def tile_pair(key):
    tiles_dev = (LOC_RB + REM_RB) * RB_DEV
    rows_local = jax.random.randint(jax.random.fold_in(key, 21), (TILES,), 0, RB_DEV)
    device = jnp.arange(TILES) // tiles_dev
    blocks = device * RB_DEV + rows_local
    keep = (jax.random.uniform(jax.random.fold_in(key, 31), (BLOCKS, B)) >= 0.0625).astype(jnp.float32)
    per_row = jnp.exp(jax.random.uniform(jax.random.fold_in(key, 32), (TILES,), minval=math.log(0.5), maxval=math.log(2.5)))
    density = per_row / B
    base = jax.random.fold_in(key, 33)

    def single(index):
        level = jax.random.uniform(jax.random.fold_in(base, index), (B, B))
        dense = density[index]
        alive = keep[blocks[index]][:, None]
        real_part = (level < 0.3 * dense).astype(jnp.float32) * alive
        upper = ((level >= 0.3 * dense) & (level < 0.65 * dense)).astype(jnp.float32)
        lower_part = ((level >= 0.65 * dense) & (level < dense)).astype(jnp.float32)
        return (real_part, (upper - lower_part) * alive)
    return lax.map(single, jnp.arange(TILES))


def draw_tile_real(key, part):
    return tile_pair(key)[0].astype(jnp.bfloat16)


def draw_tile_imag(key, part):
    return tile_pair(key)[1].astype(jnp.bfloat16)


def draw_tile_rows(key, part):
    return jax.random.randint(jax.random.fold_in(key, 21), (TILES,), 0, RB_DEV).astype(jnp.int32)


def draw_tile_slots(key, part):
    tiles_dev = (LOC_RB + REM_RB) * RB_DEV
    local_count = LOC_RB * RB_DEV
    nblk = BLOCKS // RB_DEV
    index = jnp.arange(TILES)
    device = index // tiles_dev
    within = index % tiles_dev
    own = jax.random.randint(jax.random.fold_in(key, 41), (TILES,), 0, RB_DEV)
    offset = jax.random.randint(jax.random.fold_in(key, 42), (TILES,), 1, nblk)
    later = within - local_count
    offset = jnp.where(later == 0, 1, jnp.where(later == 1, nblk // 2, jnp.where(later == 2, nblk - 1, offset)))
    owner = (device + offset) % nblk
    return jnp.where(within < local_count, own, RB_DEV + owner).astype(jnp.int32)


def draw_y_start(key, part):
    node_level = jnp.exp(jax.random.uniform(jax.random.fold_in(key, 61), (NODES,), minval=0.0, maxval=math.log(10.0)))
    vec_level = jnp.exp(jax.random.uniform(jax.random.fold_in(key, 62), (VEC2,), minval=0.0, maxval=math.log(10.0)))
    position = jnp.arange(NODES).astype(jnp.float32) / NODES
    noise = jax.random.normal(jax.random.fold_in(key, 63), (VEC2, NODES))
    ramp = jnp.exp(position * math.log(3.0))
    values = noise * vec_level[:, None] * (node_level * ramp)[None, :]
    return values.astype(jnp.float32)


def with_ends(values, key, low, top_value):
    place = [jax.random.randint(jax.random.fold_in(key, axis), (), 0, length) for axis, length in enumerate(values.shape)]
    main_axis = values.shape.index(max(values.shape))
    beside = place[:main_axis] + [(place[main_axis] + 1) % values.shape[main_axis]] + place[main_axis + 1:]
    return values.at[tuple(place)].set(low).at[tuple(beside)].set(top_value)


def setup_inputs(seed: int = 0) -> dict:
    seeds = jax.random.split(jax.random.key(seed), 7)
    return {
        "y_start": draw_y_start(jax.random.fold_in(seeds[6], 71), 0),
        "tile_real": draw_tile_real(jax.random.fold_in(seeds[6], 71), 0),
        "tile_imag": draw_tile_imag(jax.random.fold_in(seeds[6], 71), 0),
        "tile_rows": draw_tile_rows(jax.random.fold_in(seeds[6], 71), 0),
        "tile_slots": draw_tile_slots(jax.random.fold_in(seeds[6], 71), 0),
        "fetch_pick": with_ends(jax.random.randint(seeds[5], (BLOCKS // RB_DEV, BLOCKS // RB_DEV), 0, RB_DEV), jax.random.fold_in(seeds[5], 1), 0, RB_DEV - 1).astype(jnp.int32),
    }


center = 1.25
half_width = 0.75

def turn(values):
    pairs = values.reshape((values.shape[0] // 2, 2) + values.shape[1:])
    return jnp.stack([-pairs[:, 1], pairs[:, 0]], axis=1).reshape(values.shape)

def reference(y_start, tile_real, tile_imag, tile_rows, tile_slots, fetch_pick):
    nblk = BLOCKS // RB_DEV
    device = jnp.arange(TILES, dtype=jnp.int32) // TILES_DEV
    row_block = (device * RB_DEV + tile_rows).astype(jnp.int32)
    owner = jnp.clip(tile_slots - RB_DEV, 0, nblk - 1).astype(jnp.int32)
    remote_block = owner * RB_DEV + fetch_pick[device, owner]
    col_block = jnp.where(tile_slots < RB_DEV, device * RB_DEV + tile_slots, remote_block).astype(jnp.int32)
    real_dev = tile_real.reshape(nblk, TILES_DEV, B, B)
    imag_dev = tile_imag.reshape(nblk, TILES_DEV, B, B)
    rows_dev = row_block.reshape(nblk, TILES_DEV)
    cols_dev = col_block.reshape(nblk, TILES_DEV)

    def count(total, items):
        real_part, imag_part, rows_here = items
        counted = lax.optimization_barrier(jnp.sum(jnp.abs(real_part).astype(jnp.float32) + jnp.abs(imag_part).astype(jnp.float32), axis=2))
        return (total.at[rows_here].add(counted), None)
    degree, _ = lax.scan(count, jnp.zeros((BLOCKS, B), jnp.float32), (real_dev, imag_dev, rows_dev))
    scale = (1.0 / jnp.sqrt(jnp.maximum(degree, 1.0))).reshape(NODES)

    def operate(field):
        sent = (field * scale[None, :]).astype(jnp.bfloat16).reshape(VEC2, BLOCKS, B)

        def add_tiles(carry, items):
            real_part, imag_part, rows_here, cols_here = items
            picked = sent[:, cols_here, :].astype(jnp.float32)
            prod_re = jnp.einsum('ctb,tab->cta', picked, real_part.astype(jnp.float32))
            prod_im = jnp.einsum('ctb,tab->cta', picked, imag_part.astype(jnp.float32))
            return ((carry[0].at[:, rows_here, :].add(prod_re), carry[1].at[:, rows_here, :].add(prod_im)), None)
        empty = jnp.zeros((VEC2, BLOCKS, B), jnp.float32)
        (acc_re, acc_im), _ = lax.scan(add_tiles, (empty, empty), (real_dev, imag_dev, rows_dev, cols_dev))
        applied = (acc_re + turn(acc_im)).reshape(VEC2, NODES) * scale[None, :]
        return ((1.0 - center) * field - applied) / half_width
    previous = y_start
    current = operate(y_start)
    for step in range(1, STEPS):
        following = 2.0 * operate(current) - previous
        previous, current = (current, following)
    gram = jnp.dot(current, current.T, precision=lax.Precision.HIGHEST)
    gram = gram + turn(turn(gram).T).T
    lower = jnp.linalg.cholesky(gram)
    solved = jax.scipy.linalg.solve_triangular(lower, current, lower=True)
    return solved * math.sqrt(NODES)
```

```python
import math

import jax
import jax.numpy as jnp
from jax import lax
from jax.experimental import pallas as pl
from jax.experimental.pallas import tpu as pltpu
from jax.sharding import PartitionSpec as P

STEPS = 4
NEAR = 16
TILES = 96
RB = 8
GROUP = 32
HALF = 16
ORDER = 256
NZ, NY = 8, 4
CHUNK = 8
UNROLL = 16
MESH = pl.DeviceIdType.MESH

center = 1.25
half_width = 0.75

Z_PLACE = (0, 2, 4, 6, 7, 5, 3, 1)
Z_OFFSET = (0, 7, 1, 6, 2, 5, 3, 4)
GROUPS = ((0, 1), (1, 2), (3, 2), (5, 2), (7, 1))


def turn(values):
    pairs = values.reshape((values.shape[0] // 2, 2) + values.shape[1:])
    return jnp.stack([-pairs[:, 1], pairs[:, 0]], axis=1).reshape(values.shape)


def filter_kernel(
    prev_ref, last_ref, src_ref, y_ref, picks_ref, real_ref, imag_ref, out_ref, *scratch
):
    own = scratch[0:2]
    zbuf = (None,) + tuple(scratch[2 + 2 * i : 4 + 2 * i] for i in range(7))
    arr = scratch[16:18]
    stage = scratch[18:20]
    (
        weights, raw, sums, degs, scale, field, before,
        pick_in, pick_s,
        raw_sem, pick_send, pick_recv, pick_loc, z_send, z_recv, y_send, y_recv,
    ) = scratch[20:]
    me = lax.axis_index("blk")
    zi, yi, ci = me // 8, (me // 2) % NY, me % 2
    up = ((zi + 1) % NZ) * 8 + yi * 2 + ci
    down = ((zi + NZ - 1) % NZ) * 8 + yi * 2 + ci

    def partner(j):
        dy, dc = j // 2, j % 2
        return zi * 8 + ((yi + dy) % NY) * 2 + (ci + dc) % 2

    barrier = pltpu.get_barrier_semaphore()
    for other in [up, down] + [partner(j) for j in range(1, 8)]:
        pl.semaphore_signal(barrier, inc=1, device_id={"blk": other}, device_id_type=MESH)

    def raw_copies(k):
        return [
            pltpu.make_async_copy(
                ref.at[pl.ds(k * CHUNK, CHUNK)], raw.at[k % 2, i], raw_sem.at[k % 2, i]
            )
            for i, ref in enumerate((real_ref, imag_ref))
        ]

    for copy in raw_copies(0):
        copy.start()
    pl.semaphore_wait(barrier, 9)

    def pick_copy(j):
        return pltpu.make_async_remote_copy(
            src_ref=picks_ref,
            dst_ref=pick_in.at[j],
            send_sem=pick_send.at[j],
            recv_sem=pick_recv.at[j],
            device_id={"blk": partner(j)},
            device_id_type=MESH,
        )

    for j in range(1, 8):
        pick_copy(j).start()

    degs[0] = jnp.zeros((8, ORDER), jnp.float32)
    sums[0] = jnp.zeros((GROUP, ORDER), jnp.float32)
    ones = jnp.ones((8, ORDER), jnp.bfloat16)

    def load_chunk(k, carry):
        @pl.when(k + 1 < TILES // CHUNK)
        def _():
            for copy in raw_copies(k + 1):
                copy.start()

        for copy in raw_copies(k):
            copy.wait()

        def one(i, c):
            t = k * CHUNK + i
            re_t = raw[k % 2, 0, i].T
            im_t = raw[k % 2, 1, i].T
            weights[t, 0:ORDER] = re_t
            weights[t, ORDER : 2 * ORDER] = im_t
            count = jnp.dot(ones, jnp.abs(re_t) + jnp.abs(im_t), preferred_element_type=jnp.float32)
            degs[t + 1] = count + degs[prev_ref[t]]
            return c

        return lax.fori_loop(0, CHUNK, one, carry, unroll=4)

    lax.fori_loop(0, TILES // CHUNK, load_chunk, 0)
    for r in range(RB):
        scale[r] = 1.0 / jnp.sqrt(jnp.maximum(degs[last_ref[r]], 1.0))

    pick_in[0] = picks_ref[...]
    for j in range(1, 8):
        pick_copy(j).wait()
    to_smem = pltpu.make_async_copy(pick_in, pick_s, pick_loc.at[0])
    to_smem.start()
    to_smem.wait()

    field[...] = y_ref[...]

    def z_copy(par, way, hop, half):
        place_in = 2 * hop - 1 + way if hop > 0 else 0
        place_out = 2 * hop + 1 + way if hop < 3 else 7
        source = own[par] if hop == 0 else zbuf[place_in][par]
        part = pl.ds(half * 4, 4)
        return pltpu.make_async_remote_copy(
            src_ref=source.at[part],
            dst_ref=zbuf[place_out][par].at[part],
            send_sem=z_send.at[par, way, hop, half],
            recv_sem=z_recv.at[par, way, hop, half],
            device_id={"blk": down if way else up},
            device_id_type=MESH,
        )

    def y_copy(par, j, g):
        first, count = GROUPS[g]
        return pltpu.make_async_remote_copy(
            src_ref=stage[par].at[j, pl.ds(first, count)],
            dst_ref=arr[par].at[j, pl.ds(first, count)],
            send_sem=y_send.at[par, j, g],
            recv_sem=y_recv.at[par, j, g],
            device_id={"blk": partner(j)},
            device_id_type=MESH,
        )

    def hand_on(par, g):
        first, count = GROUPS[g]
        for j in (2, 3, 6, 7, 4, 5, 1, 0):
            if j == 0 and g == 0:
                continue
            for k in range(first, first + count):
                source = own[par] if k == 0 else zbuf[k][par]
                owner = ((zi + Z_OFFSET[k]) % NZ) * 8 + yi * 2 + ci
                row = ((4 - j // 2) % 4) * 2 + j % 2
                block = source[pick_s[row, 0, owner]]
                if j == 0:
                    arr[par][0, k] = block
                else:
                    stage[par][j, k] = block
            if j != 0:
                y_copy(par, j, g).start()

    def product(block, t):
        lower = block[HALF:GROUP]
        left = jnp.concatenate([block, jnp.concatenate([-lower, block[0:HALF]], axis=0)], axis=1)
        sums[t + 1] = sums[prev_ref[t]] + jnp.dot(
            left, weights[t], preferred_element_type=jnp.float32
        )

    for step in range(STEPS):
        par = step % 2
        for r in range(RB):
            s4 = jnp.concatenate([scale[r]] * 4, axis=0)
            own[par][r] = (field[r] * s4).astype(jnp.bfloat16)
        for half in range(2):
            for way in range(2):
                z_copy(par, way, 0, half).start()
        hand_on(par, 0)

        def near(t, c):
            product(own[par][src_ref[t]], t)
            return c

        lax.fori_loop(0, NEAR, near, 0, unroll=UNROLL)
        for hop in range(1, 4):
            for half in range(2):
                for way in range(2):
                    z_copy(par, way, hop - 1, half).wait_recv()
                    if hop < 3 or half == way:
                        z_copy(par, way, hop, half).start()
            hand_on(par, hop)
        for way in range(2):
            z_copy(par, way, 3, way).wait_recv()
        hand_on(par, 4)
        for g in range(5):
            for j in range(1, 8):
                y_copy(par, j, g).wait_recv()

        def far(t, c):
            place = src_ref[t]
            product(arr[par][place // 8, place % 8], t)
            return c

        lax.fori_loop(NEAR, TILES, far, 0, unroll=UNROLL)
        for r in range(RB):
            s4 = jnp.concatenate([scale[r]] * 4, axis=0)
            now = field[r]
            moved = ((1.0 - center) * now - sums[last_ref[r]] * s4) / half_width
            if step > 0:
                moved = 2.0 * moved - before[r]
            if step < STEPS - 1:
                before[r] = now
                field[r] = moved
            else:
                out_ref[r] = moved
        for hop in range(4):
            for way in range(2):
                for half in range(2):
                    if hop < 3 or half == way:
                        z_copy(par, way, hop, half).wait_send()
        for g in range(5):
            for j in range(1, 8):
                y_copy(par, j, g).wait_send()


def chebyshev(y_start, tile_real, tile_imag, tile_rows, tile_slots, fetch_pick):
    me = lax.axis_index("blk")
    zi, yi, ci = me // 8, (me // 2) % NY, me % 2
    order = jnp.arange(TILES, dtype=jnp.int32)
    same = (tile_rows[:, None] == tile_rows[None, :]) & (order[None, :] < order[:, None])
    prev = jnp.max(jnp.where(same, order[None, :] + 1, 0), axis=1)
    here = tile_rows[None, :] == jnp.arange(RB, dtype=jnp.int32)[:, None]
    last = jnp.max(jnp.where(here, order[None, :] + 1, 0), axis=1)
    owner = tile_slots - RB
    zp, yp, cp = owner // 8, (owner // 2) % NY, owner % 2
    dz = (zp - zi) % NZ
    place = jnp.where(
        dz == 0, 0, jnp.where(dz < 4, 2 * dz, jnp.where(dz == 4, 7, 2 * (8 - dz) - 1))
    )
    j = ((yi - yp) % NY) * 2 + (ci + cp) % 2
    src = jnp.where(order < NEAR, tile_slots, j * 8 + place)
    picks = jnp.pad(fetch_pick, ((0, 7), (0, 64)))
    block = (RB, GROUP, ORDER)
    split = y_start.reshape(HALF, 2, RB, ORDER).transpose(2, 1, 0, 3).reshape(block)
    done = pl.pallas_call(
        filter_kernel,
        name="filter",
        out_shape=jax.ShapeDtypeStruct(block, jnp.float32),
        in_specs=[pl.BlockSpec(memory_space=pltpu.SMEM)] * 3
        + [pl.BlockSpec(memory_space=pltpu.VMEM)] * 2
        + [pl.BlockSpec(memory_space=pl.ANY)] * 2,
        out_specs=pl.BlockSpec(memory_space=pltpu.VMEM),
        scratch_shapes=[pltpu.VMEM(block, jnp.bfloat16)] * 16
        + [pltpu.VMEM((8,) + block, jnp.bfloat16)] * 4
        + [
            pltpu.VMEM((TILES, 2 * ORDER, ORDER), jnp.bfloat16),
            pltpu.VMEM((2, 2, CHUNK, ORDER, ORDER), jnp.bfloat16),
            pltpu.VMEM((TILES + 1, GROUP, ORDER), jnp.float32),
            pltpu.VMEM((TILES + 1, 8, ORDER), jnp.float32),
            pltpu.VMEM((RB, 8, ORDER), jnp.float32),
            pltpu.VMEM(block, jnp.float32),
            pltpu.VMEM(block, jnp.float32),
            pltpu.VMEM((8, 8, 128), jnp.int32),
            pltpu.SMEM((8, 8, 128), jnp.int32),
            pltpu.SemaphoreType.DMA((2, 2)),
            pltpu.SemaphoreType.DMA((8,)),
            pltpu.SemaphoreType.DMA((8,)),
            pltpu.SemaphoreType.DMA((1,)),
            pltpu.SemaphoreType.DMA((2, 2, 4, 2)),
            pltpu.SemaphoreType.DMA((2, 2, 4, 2)),
            pltpu.SemaphoreType.DMA((2, 8, 5)),
            pltpu.SemaphoreType.DMA((2, 8, 5)),
        ],
        compiler_params=pltpu.CompilerParams(
            collective_id=0, has_side_effects=True, vmem_limit_bytes=58 << 20
        ),
    )(prev, last, src, split, picks, tile_real, tile_imag)
    return done.reshape(RB, 2, HALF, ORDER).transpose(2, 1, 0, 3).reshape(y_start.shape)


def per_device(y_start, tile_real, tile_imag, tile_rows, tile_slots, fetch_pick):
    group, rows = y_start.shape
    nblk = lax.axis_size("blk")
    current = chebyshev(y_start, tile_real, tile_imag, tile_rows, tile_slots, fetch_pick)
    gathered = lax.all_gather(current, "col", axis=0, tiled=True)
    partial_gram = jnp.dot(gathered, gathered.T, precision=lax.Precision.HIGHEST)
    gram = lax.psum(partial_gram, "blk")
    gram = gram + turn(turn(gram).T).T
    lower = jnp.linalg.cholesky(gram)
    solved = jax.scipy.linalg.solve_triangular(lower, gathered, lower=True)
    mine = lax.dynamic_slice_in_dim(solved, lax.axis_index("col") * group, group, 0)
    return mine * math.sqrt(rows * nblk)


def solution(mesh):
    return jax.shard_map(
        per_device,
        mesh=mesh,
        in_specs=(
            P("col", "blk"),
            P("blk", None, None),
            P("blk", None, None),
            P("blk"),
            P("blk"),
            P("blk", None),
        ),
        out_specs=P("col", "blk"),
        check_vma=False,
    )
```

```python
import math

import jax
import jax.numpy as jnp
from jax import lax
from jax.experimental import pallas as pl
from jax.experimental.pallas import tpu as pltpu
from jax.sharding import PartitionSpec as P

STEPS = 4
NEAR = 16
TILES = 96
RB = 8
GROUP = 32
HALF = 16
ORDER = 256
NZ, NY, NX = 8, 4, 4
PLANE = 32
VEC = 64
NODES = 131072
CHUNK = 8
UNROLL = 16
MESH = pl.DeviceIdType.MESH

center = 1.25
half_width = 0.75

Z_PLACE = (0, 2, 4, 6, 7, 5, 3, 1)
Z_OFFSET = (0, 7, 1, 6, 2, 5, 3, 4)
GROUPS = ((0, 1), (1, 2), (3, 2), (5, 2), (7, 1))


def filter_kernel(rows_ref, slots_ref, y_ref, picks_ref, real_ref, imag_ref, out_ref, *scratch):
    own = scratch[0:2]
    zbuf = (None,) + tuple(scratch[2 + 2 * i : 4 + 2 * i] for i in range(7))
    arr = scratch[16:18]
    stage = scratch[18:20]
    (
        weights, raw, sums, degs, scale, field, before,
        pick_in, pick_s, prev_ref, last_ref, src_ref,
        quarter, joined, pieces, by_z, by_plane, total, elim, inverse, solver, solved, landed, pick_row,
        raw_sem, pick_send, pick_recv, pick_loc, z_send, z_recv, y_send, y_recv,
        x_send, x_recv, a_send, a_recv, b_send, b_recv, c_send, c_recv, e_send, e_recv,
    ) = scratch[20:]
    xi = lax.axis_index("col")
    me = lax.axis_index("blk")
    zi, yi, ci = me // 8, (me // 2) % NY, me % 2
    up = ((zi + 1) % NZ) * 8 + yi * 2 + ci
    down = ((zi + NZ - 1) % NZ) * 8 + yi * 2 + ci

    def partner(j):
        dy, dc = j // 2, j % 2
        return zi * 8 + ((yi + dy) % NY) * 2 + (ci + dc) % 2

    barrier = pltpu.get_barrier_semaphore()
    for dz in range(1, NZ):
        pl.semaphore_signal(
            barrier, inc=1, device_id={"blk": (me + 8 * dz) % 64}, device_id_type=MESH
        )

    def plane_peer(m):
        dx, dy, dc = m // 8, (m // 2) % NY, m % 2
        return {
            "blk": zi * 8 + ((yi + dy) % NY) * 2 + (ci + dc) % 2,
            "col": (xi + dx) % NX,
        }

    def greet(m, carry):
        pl.semaphore_signal(barrier, inc=1, device_id=plane_peer(m), device_id_type=MESH)
        return carry

    lax.fori_loop(1, PLANE, greet, 0)

    def raw_copies(k):
        return [
            pltpu.make_async_copy(
                ref.at[pl.ds(k * CHUNK, CHUNK)], raw.at[k % 2, i], raw_sem.at[k % 2, i]
            )
            for i, ref in enumerate((real_ref, imag_ref))
        ]

    for copy in raw_copies(0):
        copy.start()
    pl.semaphore_wait(barrier, NZ - 1 + PLANE - 1)

    pick_row[...] = jnp.zeros((8, 128), jnp.int32)
    pick_row[0:1, 0:64] = picks_ref[...]

    def pick_copy(j):
        return pltpu.make_async_remote_copy(
            src_ref=pick_row,
            dst_ref=pick_in.at[j],
            send_sem=pick_send.at[j],
            recv_sem=pick_recv.at[j],
            device_id={"blk": partner(j)},
            device_id_type=MESH,
        )

    for j in range(1, 8):
        pick_copy(j).start()

    degs[0] = jnp.zeros((8, ORDER), jnp.float32)
    sums[0] = jnp.zeros((GROUP, ORDER), jnp.float32)
    ones = jnp.ones((8, ORDER), jnp.bfloat16)

    def load_chunk(k, carry):
        @pl.when(k + 1 < TILES // CHUNK)
        def _():
            for copy in raw_copies(k + 1):
                copy.start()

        for copy in raw_copies(k):
            copy.wait()

        def one(i, c):
            t = k * CHUNK + i
            row, slot = rows_ref[t], slots_ref[t]
            before_t = jnp.int32(0)
            for q in range(RB):
                last_q = last_ref[q]
                before_t = jnp.where(row == q, last_q, before_t)
                last_ref[q] = jnp.where(row == q, t + 1, last_q)
            prev_ref[t] = before_t
            owner = slot - RB
            dz = (owner // 8 - zi + NZ) % NZ
            place = jnp.where(dz < 4, 2 * dz, jnp.where(dz == 4, 7, 15 - 2 * dz))
            j = ((yi - (owner // 2) % NY + NY) % NY) * 2 + (ci + owner) % 2
            src_ref[t] = jnp.where(t < NEAR, slot, j * 8 + place)
            re_t = raw[k % 2, 0, i].T
            im_t = raw[k % 2, 1, i].T
            weights[t, 0:ORDER] = re_t
            weights[t, ORDER : 2 * ORDER] = im_t
            count = jnp.dot(ones, jnp.abs(re_t) + jnp.abs(im_t), preferred_element_type=jnp.float32)
            degs[t + 1] = count + degs[before_t]
            return c

        return lax.fori_loop(0, CHUNK, one, carry, unroll=4)

    for r in range(RB):
        last_ref[r] = jnp.int32(0)
    lax.fori_loop(0, TILES // CHUNK, load_chunk, 0)
    for r in range(RB):
        scale[r] = 1.0 / jnp.sqrt(jnp.maximum(degs[last_ref[r]], 1.0))

    pick_in[0] = pick_row[...]
    for j in range(1, 8):
        pick_copy(j).wait()
    to_smem = pltpu.make_async_copy(pick_in, pick_s, pick_loc.at[0])
    to_smem.start()
    to_smem.wait()

    to_row = lax.broadcasted_iota(jnp.int32, (GROUP, GROUP), 0)
    from_row = lax.broadcasted_iota(jnp.int32, (GROUP, GROUP), 1)
    part_first = (from_row == (to_row % HALF) * 2 + to_row // HALF).astype(jnp.float32)
    for r in range(RB):
        field[r] = jnp.dot(
            part_first,
            y_ref[:, r * ORDER : (r + 1) * ORDER],
            precision=lax.Precision.HIGHEST,
            preferred_element_type=jnp.float32,
        )

    def z_copy(par, way, hop, half):
        place_in = 2 * hop - 1 + way if hop > 0 else 0
        place_out = 2 * hop + 1 + way if hop < 3 else 7
        source = own[par] if hop == 0 else zbuf[place_in][par]
        part = pl.ds(half * 4, 4)
        return pltpu.make_async_remote_copy(
            src_ref=source.at[part],
            dst_ref=zbuf[place_out][par].at[part],
            send_sem=z_send.at[par, way, hop, half],
            recv_sem=z_recv.at[par, way, hop, half],
            device_id={"blk": down if way else up},
            device_id_type=MESH,
        )

    def y_copy(par, j, g):
        first, count = GROUPS[g]
        return pltpu.make_async_remote_copy(
            src_ref=stage[par].at[j, pl.ds(first, count)],
            dst_ref=arr[par].at[j, pl.ds(first, count)],
            send_sem=y_send.at[par, j, g],
            recv_sem=y_recv.at[par, j, g],
            device_id={"blk": partner(j)},
            device_id_type=MESH,
        )

    def hand_on(par, g):
        first, count = GROUPS[g]
        for j in (2, 3, 6, 7, 4, 5, 1, 0):
            if j == 0 and g == 0:
                continue
            for k in range(first, first + count):
                source = own[par] if k == 0 else zbuf[k][par]
                owner = ((zi + Z_OFFSET[k]) % NZ) * 8 + yi * 2 + ci
                row = ((4 - j // 2) % 4) * 2 + j % 2
                block = source[pick_s[row, 0, owner]]
                if j == 0:
                    arr[par][0, k] = block
                else:
                    stage[par][j, k] = block
            if j != 0:
                y_copy(par, j, g).start()

    def product(block, t):
        lower = block[HALF:GROUP]
        left = jnp.concatenate([block, jnp.concatenate([-lower, block[0:HALF]], axis=0)], axis=1)
        sums[t + 1] = sums[prev_ref[t]] + jnp.dot(
            left, weights[t], preferred_element_type=jnp.float32
        )

    for step in range(STEPS):
        par = step % 2
        for r in range(RB):
            s4 = jnp.concatenate([scale[r]] * 4, axis=0)
            own[par][r] = (field[r] * s4).astype(jnp.bfloat16)
        for half in range(2):
            for way in range(2):
                z_copy(par, way, 0, half).start()
        hand_on(par, 0)

        def near(t, c):
            product(own[par][src_ref[t]], t)
            return c

        lax.fori_loop(0, NEAR, near, 0, unroll=UNROLL)
        for hop in range(1, 4):
            for half in range(2):
                for way in range(2):
                    z_copy(par, way, hop - 1, half).wait_recv()
                    if hop < 3 or half == way:
                        z_copy(par, way, hop, half).start()
            hand_on(par, hop)
        for way in range(2):
            z_copy(par, way, 3, way).wait_recv()
        hand_on(par, 4)
        for g in range(5):
            for j in range(1, 8):
                y_copy(par, j, g).wait_recv()

        def far(t, c):
            place = src_ref[t]
            product(arr[par][place // 8, place % 8], t)
            return c

        lax.fori_loop(NEAR, TILES, far, 0, unroll=UNROLL)
        for r in range(RB):
            s4 = jnp.concatenate([scale[r]] * 4, axis=0)
            now = field[r]
            moved = ((1.0 - center) * now - sums[last_ref[r]] * s4) / half_width
            if step > 0:
                moved = 2.0 * moved - before[r]
            before[r] = now
            field[r] = moved
        for hop in range(4):
            for way in range(2):
                for half in range(2):
                    if hop < 3 or half == way:
                        z_copy(par, way, hop, half).wait_send()
        for g in range(5):
            for j in range(1, 8):
                y_copy(par, j, g).wait_send()

    def x_copy(dx):
        to = (xi + dx) % NX
        return pltpu.make_async_remote_copy(
            src_ref=field.at[pl.ds(to * 2, 2)],
            dst_ref=quarter.at[xi],
            send_sem=x_send.at[dx],
            recv_sem=x_recv.at[dx],
            device_id={"col": to},
            device_id_type=MESH,
        )

    for dx in (2, 1, 3):
        x_copy(dx).start()
    quarter[xi] = field[pl.ds(xi * 2, 2)]
    for dx in range(1, NX):
        x_copy(dx).wait()
    for b in range(2):
        cols = slice(b * ORDER, (b + 1) * ORDER)
        for q in range(NX):
            joined[q * HALF : (q + 1) * HALF, cols] = quarter[q, b, 0:HALF]
            joined[VEC + q * HALF : VEC + (q + 1) * HALF, cols] = quarter[q, b, HALF:GROUP]

    gram = jnp.zeros((VEC, 2 * VEC), jnp.float32)
    for b in range(2):
        cols = slice(b * ORDER, (b + 1) * ORDER)
        top, low = joined[0:VEC, cols], joined[VEC : 2 * VEC, cols]
        right = jnp.concatenate(
            [jnp.concatenate([top, low], axis=1), jnp.concatenate([-low, top], axis=1)], axis=0
        )
        gram += lax.dot_general(
            jnp.concatenate([top, low], axis=1),
            right,
            (((1,), (1,)), ((), ())),
            precision=lax.Precision.HIGHEST,
            preferred_element_type=jnp.float32,
        )
    for i in range(8):
        pieces[i] = gram[i * 8 : (i + 1) * 8]

    def a_copy(dz):
        to = (zi + dz) % NZ
        return pltpu.make_async_remote_copy(
            src_ref=pieces.at[to],
            dst_ref=by_z.at[zi],
            send_sem=a_send.at[dz],
            recv_sem=a_recv.at[dz],
            device_id={"blk": (me + 8 * dz) % 64},
            device_id_type=MESH,
        )

    for dz in range(1, NZ):
        a_copy(dz).start()
    by_z[zi] = pieces[zi]
    for dz in range(1, NZ):
        a_copy(dz).wait()
    mine = by_z[0]
    for i in range(1, NZ):
        mine += by_z[i]
    place = xi * 8 + yi * 2 + ci
    by_plane[place] = mine

    def b_copy(m):
        return pltpu.make_async_remote_copy(
            src_ref=by_plane.at[place],
            dst_ref=by_plane.at[place],
            send_sem=b_send.at[m],
            recv_sem=b_recv.at[m],
            device_id=plane_peer(m),
            device_id_type=MESH,
        )

    def b_start(m, carry):
        b_copy(m).start()
        return carry

    def b_wait(m, carry):
        b_copy(m).wait()
        return carry

    lax.fori_loop(1, PLANE, b_start, 0)
    lax.fori_loop(1, PLANE, b_wait, 0)
    mine = by_plane[0]
    for i in range(1, PLANE):
        mine += by_plane[i]
    total[zi] = mine

    def c_copy(dz):
        return pltpu.make_async_remote_copy(
            src_ref=total.at[zi],
            dst_ref=total.at[zi],
            send_sem=c_send.at[dz],
            recv_sem=c_recv.at[dz],
            device_id={"blk": (me + 8 * dz) % 64},
            device_id_type=MESH,
        )

    for dz in range(1, NZ):
        c_copy(dz).start()
    for dz in range(1, NZ):
        c_copy(dz).wait()

    wide = (VEC, 2 * VEC)
    sub = lax.broadcasted_iota(jnp.int32, wide, 0)
    lane = lax.broadcasted_iota(jnp.int32, wide, 1)
    sign = jnp.where(lane < VEC, -1.0, 1.0).astype(jnp.float32)
    for i in range(8):
        elim[i * 8 : (i + 1) * 8] = total[i]
    inverse[...] = (lane == sub).astype(jnp.float32)

    def eliminate(k, carry):
        a, v = elim[...], inverse[...]
        a_row = jnp.broadcast_to(elim[pl.ds(k, 1)], wide)
        v_row = jnp.broadcast_to(inverse[pl.ds(k, 1)], wide)
        pivot = jnp.sum(jnp.where(lane == k, a_row, 0.0), axis=1, keepdims=True)
        col_re = jnp.sum(jnp.where(lane == k, a, 0.0), axis=1, keepdims=True)
        col_im = jnp.sum(jnp.where(lane == k + VEC, a, 0.0), axis=1, keepdims=True)
        below = sub > k
        m_re = jnp.where(below, col_re / pivot, 0.0)
        m_im = jnp.where(below, col_im / pivot, 0.0)
        a_turned = pltpu.roll(a_row, VEC, 1) * sign
        v_turned = pltpu.roll(v_row, VEC, 1) * sign
        elim[...] = a - m_re * a_row - m_im * a_turned
        inverse[...] = v - m_re * v_row - m_im * v_turned
        return carry

    lax.fori_loop(0, VEC, eliminate, 0)
    pivots = jnp.sum(jnp.where(lane == sub, elim[...], 0.0), axis=1, keepdims=True)
    scaled = inverse[...] * (math.sqrt(NODES) / jnp.sqrt(pivots))
    solver[pl.ds(0, VEC, stride=2), :] = -sign * scaled
    solver[pl.ds(1, VEC, stride=2), :] = pltpu.roll(scaled, VEC, 1)

    def e_copy(dx):
        to = (xi + dx) % NX
        return pltpu.make_async_remote_copy(
            src_ref=solved.at[to],
            dst_ref=landed.at[xi],
            send_sem=e_send.at[dx],
            recv_sem=e_recv.at[dx],
            device_id={"col": to},
            device_id_type=MESH,
        )

    for dx in (2, 1, 3, 0):
        to = (xi + dx) % NX
        part = jnp.dot(
            solver[pl.ds(to * GROUP, GROUP)],
            joined[...],
            precision=lax.Precision.HIGHEST,
            preferred_element_type=jnp.float32,
        )
        if dx:
            solved[to] = part
            e_copy(dx).start()
        else:
            landed[xi] = part
    for dx in range(1, NX):
        e_copy(dx).wait()
    for q in range(NX):
        out_ref[:, q * 512 : (q + 1) * 512] = landed[q]


def per_device(y_start, tile_real, tile_imag, tile_rows, tile_slots, fetch_pick):
    block = (RB, GROUP, ORDER)
    tiny = (8, 8, 128)
    dma = pltpu.SemaphoreType.DMA
    return pl.pallas_call(
        filter_kernel,
        name="filter",
        out_shape=jax.ShapeDtypeStruct(y_start.shape, jnp.float32),
        in_specs=[pl.BlockSpec(memory_space=pltpu.SMEM)] * 2
        + [pl.BlockSpec(memory_space=pltpu.VMEM)] * 2
        + [pl.BlockSpec(memory_space=pl.ANY)] * 2,
        out_specs=pl.BlockSpec(memory_space=pltpu.VMEM),
        scratch_shapes=[pltpu.VMEM(block, jnp.bfloat16)] * 16
        + [pltpu.VMEM((8,) + block, jnp.bfloat16)] * 4
        + [
            pltpu.VMEM((TILES, 2 * ORDER, ORDER), jnp.bfloat16),
            pltpu.VMEM((2, 2, CHUNK, ORDER, ORDER), jnp.bfloat16),
            pltpu.VMEM((TILES + 1, GROUP, ORDER), jnp.float32),
            pltpu.VMEM((TILES + 1, 8, ORDER), jnp.float32),
            pltpu.VMEM((RB, 8, ORDER), jnp.float32),
            pltpu.VMEM(block, jnp.float32),
            pltpu.VMEM(block, jnp.float32),
            pltpu.VMEM((8, 8, 128), jnp.int32),
            pltpu.SMEM((8, 8, 128), jnp.int32),
            pltpu.SMEM((TILES,), jnp.int32),
            pltpu.SMEM((RB,), jnp.int32),
            pltpu.SMEM((TILES,), jnp.int32),
            pltpu.VMEM((NX, 2, GROUP, ORDER), jnp.float32),
            pltpu.VMEM((2 * VEC, 512), jnp.float32),
            pltpu.VMEM(tiny, jnp.float32),
            pltpu.VMEM(tiny, jnp.float32),
            pltpu.VMEM((PLANE, 8, 128), jnp.float32),
            pltpu.VMEM(tiny, jnp.float32),
            pltpu.VMEM((VEC, 2 * VEC), jnp.float32),
            pltpu.VMEM((VEC, 2 * VEC), jnp.float32),
            pltpu.VMEM((2 * VEC, 2 * VEC), jnp.float32),
            pltpu.VMEM((NX, GROUP, 512), jnp.float32),
            pltpu.VMEM((NX, GROUP, 512), jnp.float32),
            pltpu.VMEM((8, 128), jnp.int32),
            dma((2, 2)),
            dma((8,)),
            dma((8,)),
            dma((1,)),
            dma((2, 2, 4, 2)),
            dma((2, 2, 4, 2)),
            dma((2, 8, 5)),
            dma((2, 8, 5)),
            dma((NX,)),
            dma((NX,)),
            dma((NZ,)),
            dma((NZ,)),
            dma((PLANE,)),
            dma((PLANE,)),
            dma((NZ,)),
            dma((NZ,)),
            dma((NX,)),
            dma((NX,)),
        ],
        compiler_params=pltpu.CompilerParams(
            collective_id=0, has_side_effects=True, vmem_limit_bytes=60 << 20
        ),
    )(tile_rows, tile_slots, y_start, fetch_pick, tile_real, tile_imag)


def solution(mesh):
    return jax.shard_map(
        per_device,
        mesh=mesh,
        in_specs=(
            P("col", "blk"),
            P("blk", None, None),
            P("blk", None, None),
            P("blk"),
            P("blk"),
            P("blk", None),
        ),
        out_specs=P("col", "blk"),
        check_vma=False,
    )
```

```python
import math

import jax
import jax.numpy as jnp
from jax import lax
from jax.experimental import pallas as pl
from jax.experimental.pallas import tpu as pltpu
from jax.sharding import PartitionSpec as P

STEPS = 4
NEAR = 16
TILES = 96
RB = 8
GROUP = 32
HALF = 16
ORDER = 256
NZ, NY, NX = 8, 4, 4
PLANE = 32
VEC = 64
NODES = 131072
CHUNK = 8
UNROLL = 16
MESH = pl.DeviceIdType.MESH

center = 1.25
half_width = 0.75

Z_PLACE = (0, 2, 4, 6, 7, 5, 3, 1)
Z_OFFSET = (0, 7, 1, 6, 2, 5, 3, 4)
GROUPS = ((0, 1), (1, 2), (3, 2))


def filter_kernel(rows_ref, slots_ref, y_ref, picks_ref, real_ref, imag_ref, out_ref, *scratch):
    own = scratch[0:2]
    zbuf = (None,) + tuple(scratch[2 + 2 * i : 4 + 2 * i] for i in range(4))
    arr = scratch[10:12]
    stage = scratch[12:14]
    away = scratch[14:16]
    (
        weights, raw, sums, degs, scale, field, before,
        pick_in, pick_s, prev_ref, last_ref, src_ref,
        quarter, joined, pieces, by_z, by_plane, total, elim, inverse, solver, solved, landed, pick_row,
        raw_sem, pick_send, pick_recv, pick_loc, z_send, z_recv, y_send, y_recv, w_send, w_recv,
        x_send, x_recv, a_send, a_recv, b_send, b_recv, c_send, c_recv, e_send, e_recv,
    ) = scratch[16:]
    xi = lax.axis_index("col")
    me = lax.axis_index("blk")
    zi, yi, ci = me // 8, (me // 2) % NY, me % 2
    def device(dz, dy, dc):
        return ((zi + dz + NZ) % NZ) * 8 + ((yi + dy + NY) % NY) * 2 + (ci + dc) % 2

    def partner(j):
        return device(0, j // 2, j % 2)

    def reader(q):
        if q < 8:
            return 0, q // 2, q % 2
        if q < 24:
            return (1 if q < 16 else -1), (q % 8) // 2, q % 2
        return (2, q - 24, 0) if q < 28 else (-2, q - 28, 1)

    barrier = pltpu.get_barrier_semaphore()
    others = [(dz, j // 2, j % 2) for dz in (1, -1, 2, -2) for j in range(8)]
    others += [(dz, 0, 0) for dz in (3, 4, -3)]
    for other in others:
        pl.semaphore_signal(barrier, inc=1, device_id={"blk": device(*other)}, device_id_type=MESH)

    def plane_peer(m):
        dx, dy, dc = m // 8, (m // 2) % NY, m % 2
        return {
            "blk": zi * 8 + ((yi + dy) % NY) * 2 + (ci + dc) % 2,
            "col": (xi + dx) % NX,
        }

    def greet(m, carry):
        pl.semaphore_signal(barrier, inc=1, device_id=plane_peer(m), device_id_type=MESH)
        return carry

    lax.fori_loop(1, PLANE, greet, 0)

    def raw_copies(k):
        return [
            pltpu.make_async_copy(
                ref.at[pl.ds(k * CHUNK, CHUNK)], raw.at[k % 2, i], raw_sem.at[k % 2, i]
            )
            for i, ref in enumerate((real_ref, imag_ref))
        ]

    for copy in raw_copies(0):
        copy.start()
    pick_row[...] = jnp.zeros((1, 128), jnp.int32)
    pick_row[0:1, 0:64] = picks_ref[...]

    def pick_copy(q):
        dz, dy, dc = reader(q)
        return pltpu.make_async_remote_copy(
            src_ref=pick_row,
            dst_ref=pick_in.at[q],
            send_sem=pick_send.at[q],
            recv_sem=pick_recv.at[q],
            device_id={"blk": device(-dz, -dy, dc)},
            device_id_type=MESH,
        )

    degs[0] = jnp.zeros((8, ORDER), jnp.float32)
    sums[0] = jnp.zeros((GROUP, ORDER), jnp.float32)
    ones = jnp.ones((8, ORDER), jnp.bfloat16)

    def load_chunk(k, carry):
        @pl.when(k + 1 < TILES // CHUNK)
        def _():
            for copy in raw_copies(k + 1):
                copy.start()

        for copy in raw_copies(k):
            copy.wait()

        def one(i, c):
            t = k * CHUNK + i
            row, slot = rows_ref[t], slots_ref[t]
            before_t = jnp.int32(0)
            for q in range(RB):
                last_q = last_ref[q]
                before_t = jnp.where(row == q, last_q, before_t)
                last_ref[q] = jnp.where(row == q, t + 1, last_q)
            prev_ref[t] = before_t
            owner = slot - RB
            dz = (owner // 8 - zi + NZ) % NZ
            place = jnp.where(dz < 4, 2 * dz, jnp.where(dz == 4, 7, 15 - 2 * dz))
            j = ((yi - (owner // 2) % NY + NY) % NY) * 2 + (ci + owner) % 2
            src_ref[t] = jnp.where(t < NEAR, slot, j * 8 + place)
            re_t = raw[k % 2, 0, i].T
            im_t = raw[k % 2, 1, i].T
            weights[t, 0:ORDER] = re_t
            weights[t, ORDER : 2 * ORDER] = im_t
            count = jnp.dot(ones, jnp.abs(re_t) + jnp.abs(im_t), preferred_element_type=jnp.float32)
            degs[t + 1] = count + degs[before_t]
            return c

        return lax.fori_loop(0, CHUNK, one, carry, unroll=CHUNK)

    for r in range(RB):
        last_ref[r] = jnp.int32(0)
    lax.fori_loop(0, TILES // CHUNK // 2, load_chunk, 0)
    pl.semaphore_wait(barrier, len(others) + PLANE - 1)
    for q in range(1, 32):
        pick_copy(q).start()
    lax.fori_loop(TILES // CHUNK // 2, TILES // CHUNK, load_chunk, 0)
    for r in range(RB):
        scale[r] = 1.0 / jnp.sqrt(jnp.maximum(degs[last_ref[r]], 1.0))

    pick_in[0] = pick_row[...]
    for q in range(1, 32):
        pick_copy(q).wait()
    to_smem = pltpu.make_async_copy(pick_in, pick_s, pick_loc.at[0])
    to_smem.start()
    to_smem.wait()

    to_row = lax.broadcasted_iota(jnp.int32, (GROUP, GROUP), 0)
    from_row = lax.broadcasted_iota(jnp.int32, (GROUP, GROUP), 1)
    part_first = (from_row == (to_row % HALF) * 2 + to_row // HALF).astype(jnp.float32)
    for r in range(RB):
        field[r] = jnp.dot(
            part_first,
            y_ref[:, r * ORDER : (r + 1) * ORDER],
            precision=lax.Precision.HIGHEST,
            preferred_element_type=jnp.float32,
        )

    def z_copy(par, way, kind, half):
        source = own[par] if kind == 0 else zbuf[1 + way][par]
        part = pl.ds(half * 4, 4)
        return pltpu.make_async_remote_copy(
            src_ref=source.at[part],
            dst_ref=zbuf[1 + 2 * kind + way][par].at[part],
            send_sem=z_send.at[par, way, kind, half],
            recv_sem=z_recv.at[par, way, kind, half],
            device_id={"blk": device(-1 if way else 1, 0, 0)},
            device_id_type=MESH,
        )

    def w_copy(par, q):
        dz, dy, dc = reader(q)
        return pltpu.make_async_remote_copy(
            src_ref=away[par].at[q - 8],
            dst_ref=arr[par].at[dy * 2 + dc, 5 if dz == 1 else 6 if dz == -1 else 7],
            send_sem=w_send.at[par, q - 8],
            recv_sem=w_recv.at[par, q - 8],
            device_id={"blk": device(dz, dy, dc)},
            device_id_type=MESH,
        )

    def y_copy(par, j, g):
        first, count = GROUPS[g]
        return pltpu.make_async_remote_copy(
            src_ref=stage[par].at[j, pl.ds(first, count)],
            dst_ref=arr[par].at[j, pl.ds(first, count)],
            send_sem=y_send.at[par, j, g],
            recv_sem=y_recv.at[par, j, g],
            device_id={"blk": partner(j)},
            device_id_type=MESH,
        )

    def hand_on(par, g):
        first, count = GROUPS[g]
        for j in (2, 3, 6, 7, 4, 5, 1, 0):
            if j == 0 and g == 0:
                continue
            for k in range(first, first + count):
                source = own[par] if k == 0 else zbuf[k][par]
                owner = ((zi + Z_OFFSET[k]) % NZ) * 8 + yi * 2 + ci
                block = source[pick_s[j, 0, owner]]
                if j == 0:
                    arr[par][0, k] = block
                else:
                    stage[par][j, k] = block
            if j != 0:
                y_copy(par, j, g).start()

    def product(block, t):
        lower = block[HALF:GROUP]
        left = jnp.concatenate([block, jnp.concatenate([-lower, block[0:HALF]], axis=0)], axis=1)
        sums[t + 1] = sums[prev_ref[t]] + jnp.dot(
            left, weights[t], preferred_element_type=jnp.float32
        )

    before[...] = jnp.zeros_like(before)

    def apply(par, factor):
        for r in range(RB):
            s4 = jnp.concatenate([scale[r]] * 4, axis=0)
            own[par][r] = (field[r] * s4).astype(jnp.bfloat16)
        for half in range(2):
            for way in range(2):
                z_copy(par, way, 0, half).start()
        hand_on(par, 0)

        def near(t, c):
            product(own[par][src_ref[t]], t)
            return c

        lax.fori_loop(0, NEAR, near, 0, unroll=UNROLL)
        for half in range(2):
            for way in range(2):
                z_copy(par, way, 0, half).wait_recv()
                z_copy(par, way, 1, half).start()
        hand_on(par, 1)
        for half in range(2):
            for way in range(2):
                z_copy(par, way, 1, half).wait_recv()
        for first in (24, 8):
            for i in range(4 if first == 24 else 8):
                for way in range(2):
                    q = first + way * (4 if first == 24 else 8) + i
                    owner = device(2 if way else -2, 0, 0)
                    away[par][q - 8] = zbuf[3 + way][par][pick_s[q, 0, owner]]
                    w_copy(par, q).start()
        hand_on(par, 2)
        for g in range(3):
            for j in range(1, 8):
                y_copy(par, j, g).wait_recv()
        for q in range(8, 32):
            w_copy(par, q).wait_recv()

        def far(t, c):
            place = src_ref[t]
            product(arr[par][place // 8, place % 8], t)
            return c

        lax.fori_loop(NEAR, TILES, far, 0, unroll=UNROLL)
        for r in range(RB):
            s4 = jnp.concatenate([scale[r]] * 4, axis=0)
            now = field[r]
            moved = ((1.0 - center) * now - sums[last_ref[r]] * s4) / half_width
            field[r] = factor * moved - before[r]
            before[r] = now
        for kind in range(2):
            for way in range(2):
                for half in range(2):
                    z_copy(par, way, kind, half).wait_send()
        for g in range(3):
            for j in range(1, 8):
                y_copy(par, j, g).wait_send()
        for q in range(8, 32):
            w_copy(par, q).wait_send()

    def two_steps(i, c):
        apply(0, jnp.where(i == 0, 1.0, 2.0).astype(jnp.float32))
        apply(1, 2.0)
        return c

    lax.fori_loop(0, STEPS // 2, two_steps, 0)

    def x_copy(dx):
        to = (xi + dx) % NX
        return pltpu.make_async_remote_copy(
            src_ref=field.at[pl.ds(to * 2, 2)],
            dst_ref=quarter.at[xi],
            send_sem=x_send.at[dx],
            recv_sem=x_recv.at[dx],
            device_id={"col": to},
            device_id_type=MESH,
        )

    for dx in (2, 1, 3):
        x_copy(dx).start()
    quarter[xi] = field[pl.ds(xi * 2, 2)]
    for dx in range(1, NX):
        x_copy(dx).wait()
    for b in range(2):
        cols = slice(b * ORDER, (b + 1) * ORDER)
        for q in range(NX):
            joined[q * HALF : (q + 1) * HALF, cols] = quarter[q, b, 0:HALF]
            joined[VEC + q * HALF : VEC + (q + 1) * HALF, cols] = quarter[q, b, HALF:GROUP]

    gram = jnp.zeros((VEC, 2 * VEC), jnp.float32)
    for b in range(2):
        cols = slice(b * ORDER, (b + 1) * ORDER)
        top, low = joined[0:VEC, cols], joined[VEC : 2 * VEC, cols]
        right = jnp.concatenate(
            [jnp.concatenate([top, low], axis=1), jnp.concatenate([-low, top], axis=1)], axis=0
        )
        gram += lax.dot_general(
            jnp.concatenate([top, low], axis=1),
            right,
            (((1,), (1,)), ((), ())),
            precision=lax.Precision.HIGHEST,
            preferred_element_type=jnp.float32,
        )
    for i in range(8):
        pieces[i] = gram[i * 8 : (i + 1) * 8]

    def a_copy(dz):
        to = (zi + dz) % NZ
        return pltpu.make_async_remote_copy(
            src_ref=pieces.at[to],
            dst_ref=by_z.at[zi],
            send_sem=a_send.at[dz],
            recv_sem=a_recv.at[dz],
            device_id={"blk": (me + 8 * dz) % 64},
            device_id_type=MESH,
        )

    for dz in range(1, NZ):
        a_copy(dz).start()
    by_z[zi] = pieces[zi]
    for dz in range(1, NZ):
        a_copy(dz).wait()
    mine = by_z[0]
    for i in range(1, NZ):
        mine += by_z[i]
    place = xi * 8 + yi * 2 + ci
    by_plane[place] = mine

    def b_copy(m):
        return pltpu.make_async_remote_copy(
            src_ref=by_plane.at[place],
            dst_ref=by_plane.at[place],
            send_sem=b_send.at[m],
            recv_sem=b_recv.at[m],
            device_id=plane_peer(m),
            device_id_type=MESH,
        )

    def b_start(m, carry):
        b_copy(m).start()
        return carry

    def b_wait(m, carry):
        b_copy(m).wait()
        return carry

    lax.fori_loop(1, PLANE, b_start, 0)
    lax.fori_loop(1, PLANE, b_wait, 0)
    mine = by_plane[0]
    for i in range(1, PLANE):
        mine += by_plane[i]
    total[zi] = mine

    def c_copy(dz):
        return pltpu.make_async_remote_copy(
            src_ref=total.at[zi],
            dst_ref=total.at[zi],
            send_sem=c_send.at[dz],
            recv_sem=c_recv.at[dz],
            device_id={"blk": (me + 8 * dz) % 64},
            device_id_type=MESH,
        )

    for dz in range(1, NZ):
        c_copy(dz).start()
    for dz in range(1, NZ):
        c_copy(dz).wait()

    wide = (VEC, 2 * VEC)
    sub = lax.broadcasted_iota(jnp.int32, wide, 0)
    lane = lax.broadcasted_iota(jnp.int32, wide, 1)
    sign = jnp.where(lane < VEC, -1.0, 1.0).astype(jnp.float32)
    for i in range(8):
        elim[i * 8 : (i + 1) * 8] = total[i]
    inverse[...] = (lane == sub).astype(jnp.float32)

    def eliminate(k, carry):
        a, v = elim[...], inverse[...]
        a_row = jnp.broadcast_to(elim[pl.ds(k, 1)], wide)
        v_row = jnp.broadcast_to(inverse[pl.ds(k, 1)], wide)
        pivot = jnp.sum(jnp.where(lane == k, a_row, 0.0), axis=1, keepdims=True)
        col_re = jnp.sum(jnp.where(lane == k, a, 0.0), axis=1, keepdims=True)
        col_im = jnp.sum(jnp.where(lane == k + VEC, a, 0.0), axis=1, keepdims=True)
        below = sub > k
        m_re = jnp.where(below, col_re / pivot, 0.0)
        m_im = jnp.where(below, col_im / pivot, 0.0)
        a_turned = pltpu.roll(a_row, VEC, 1) * sign
        v_turned = pltpu.roll(v_row, VEC, 1) * sign
        elim[...] = a - m_re * a_row - m_im * a_turned
        inverse[...] = v - m_re * v_row - m_im * v_turned
        return carry

    lax.fori_loop(0, VEC, eliminate, 0)
    pivots = jnp.sum(jnp.where(lane == sub, elim[...], 0.0), axis=1, keepdims=True)
    scaled = inverse[...] * (math.sqrt(NODES) / jnp.sqrt(pivots))
    solver[pl.ds(0, VEC, stride=2), :] = -sign * scaled
    solver[pl.ds(1, VEC, stride=2), :] = pltpu.roll(scaled, VEC, 1)

    def e_copy(dx):
        to = (xi + dx) % NX
        return pltpu.make_async_remote_copy(
            src_ref=solved.at[to],
            dst_ref=landed.at[xi],
            send_sem=e_send.at[dx],
            recv_sem=e_recv.at[dx],
            device_id={"col": to},
            device_id_type=MESH,
        )

    for dx in (2, 1, 3, 0):
        to = (xi + dx) % NX
        part = jnp.dot(
            solver[pl.ds(to * GROUP, GROUP)],
            joined[...],
            precision=lax.Precision.HIGHEST,
            preferred_element_type=jnp.float32,
        )
        if dx:
            solved[to] = part
            e_copy(dx).start()
        else:
            landed[xi] = part
    for dx in range(1, NX):
        e_copy(dx).wait()
    for q in range(NX):
        out_ref[:, q * 512 : (q + 1) * 512] = landed[q]


def per_device(y_start, tile_real, tile_imag, tile_rows, tile_slots, fetch_pick):
    block = (RB, GROUP, ORDER)
    tiny = (8, 8, 128)
    dma = pltpu.SemaphoreType.DMA
    return pl.pallas_call(
        filter_kernel,
        name="filter",
        out_shape=jax.ShapeDtypeStruct(y_start.shape, jnp.float32),
        in_specs=[pl.BlockSpec(memory_space=pltpu.SMEM)] * 2
        + [pl.BlockSpec(memory_space=pltpu.VMEM)] * 2
        + [pl.BlockSpec(memory_space=pl.ANY)] * 2,
        out_specs=pl.BlockSpec(memory_space=pltpu.VMEM),
        scratch_shapes=[pltpu.VMEM(block, jnp.bfloat16)] * 10
        + [pltpu.VMEM((8,) + block, jnp.bfloat16)] * 4
        + [pltpu.VMEM((24,) + block[1:], jnp.bfloat16)] * 2
        + [
            pltpu.VMEM((TILES, 2 * ORDER, ORDER), jnp.bfloat16),
            pltpu.VMEM((2, 2, CHUNK, ORDER, ORDER), jnp.bfloat16),
            pltpu.VMEM((TILES + 1, GROUP, ORDER), jnp.float32),
            pltpu.VMEM((TILES + 1, 8, ORDER), jnp.float32),
            pltpu.VMEM((RB, 8, ORDER), jnp.float32),
            pltpu.VMEM(block, jnp.float32),
            pltpu.VMEM(block, jnp.float32),
            pltpu.VMEM((32, 1, 128), jnp.int32),
            pltpu.SMEM((32, 1, 128), jnp.int32),
            pltpu.SMEM((TILES,), jnp.int32),
            pltpu.SMEM((RB,), jnp.int32),
            pltpu.SMEM((TILES,), jnp.int32),
            pltpu.VMEM((NX, 2, GROUP, ORDER), jnp.float32),
            pltpu.VMEM((2 * VEC, 512), jnp.float32),
            pltpu.VMEM(tiny, jnp.float32),
            pltpu.VMEM(tiny, jnp.float32),
            pltpu.VMEM((PLANE, 8, 128), jnp.float32),
            pltpu.VMEM(tiny, jnp.float32),
            pltpu.VMEM((VEC, 2 * VEC), jnp.float32),
            pltpu.VMEM((VEC, 2 * VEC), jnp.float32),
            pltpu.VMEM((2 * VEC, 2 * VEC), jnp.float32),
            pltpu.VMEM((NX, GROUP, 512), jnp.float32),
            pltpu.VMEM((NX, GROUP, 512), jnp.float32),
            pltpu.VMEM((1, 128), jnp.int32),
            dma((2, 2)),
            dma((32,)),
            dma((32,)),
            dma((1,)),
            dma((2, 2, 2, 2)),
            dma((2, 2, 2, 2)),
            dma((2, 8, 3)),
            dma((2, 8, 3)),
            dma((2, 24)),
            dma((2, 24)),
            dma((NX,)),
            dma((NX,)),
            dma((NZ,)),
            dma((NZ,)),
            dma((PLANE,)),
            dma((PLANE,)),
            dma((NZ,)),
            dma((NZ,)),
            dma((NX,)),
            dma((NX,)),
        ],
        compiler_params=pltpu.CompilerParams(
            collective_id=0, has_side_effects=True, vmem_limit_bytes=60 << 20
        ),
    )(tile_rows, tile_slots, y_start, fetch_pick, tile_real, tile_imag)


def solution(mesh):
    return jax.shard_map(
        per_device,
        mesh=mesh,
        in_specs=(
            P("col", "blk"),
            P("blk", None, None),
            P("blk", None, None),
            P("blk"),
            P("blk"),
            P("blk", None),
        ),
        out_specs=P("col", "blk"),
        check_vma=False,
    )
```

```python
import math

import jax
import jax.numpy as jnp
from jax import lax
from jax.experimental import pallas as pl
from jax.experimental.pallas import tpu as pltpu
from jax.sharding import PartitionSpec as P

STEPS = 4
NEAR = 16
TILES = 96
RB = 8
GROUP = 32
HALF = 16
ORDER = 256
NZ, NY, NX = 8, 4, 4
PLANE = 32
VEC = 64
NODES = 131072
CHUNK = 8
UNROLL = 16
MESH = pl.DeviceIdType.MESH

center = 1.25
half_width = 0.75

Z_PLACE = (0, 2, 4, 6, 7, 5, 3, 1)
Z_OFFSET = (0, 7, 1, 6, 2, 5, 3, 4)
GROUPS = ((0, 1), (1, 2), (3, 2))


def filter_kernel(rows_ref, slots_ref, y_ref, picks_ref, real_ref, imag_ref, out_ref, *scratch):
    own = scratch[0:2]
    zbuf = (None,) + tuple(scratch[2 + 2 * i : 4 + 2 * i] for i in range(4))
    arr = scratch[10:12]
    stage = scratch[12:14]
    away = scratch[14:16]
    (
        weights, raw, sums, degs, scale, field, before,
        pick_in, pick_s, prev_ref, last_ref, src_ref,
        quarter, joined, pieces, by_z, by_plane, total, elim, inverse, solver, solved, landed, pick_row,
        raw_sem, pick_send, pick_recv, pick_loc, z_send, z_recv, y_send, y_recv, w_send, w_recv,
        x_send, x_recv, a_send, a_recv, b_send, b_recv, c_send, c_recv, e_send, e_recv,
    ) = scratch[16:]
    xi = lax.axis_index("col")
    me = lax.axis_index("blk")
    zi, yi, ci = me // 8, (me // 2) % NY, me % 2
    ids = {
        (dz, dy, dc): ((zi + dz) % NZ) * 8 + ((yi + dy) % NY) * 2 + (ci + dc) % 2
        for dz in range(NZ)
        for dy in range(NY)
        for dc in range(2)
    }

    def device(dz, dy, dc):
        return ids[dz % NZ, dy % NY, dc % 2]

    def partner(j):
        return device(0, j // 2, j % 2)

    def reader(q):
        if q < 8:
            return 0, q // 2, q % 2
        if q < 24:
            return (1 if q < 16 else -1), (q % 8) // 2, q % 2
        return (2, q - 24, 0) if q < 28 else (-2, q - 28, 1)

    barrier = pltpu.get_barrier_semaphore()
    others = [(dz, j // 2, j % 2) for dz in (1, -1, 2, -2) for j in range(8)]
    others += [(dz, 0, 0) for dz in (3, 4, -3)]
    for other in others:
        pl.semaphore_signal(barrier, inc=1, device_id={"blk": device(*other)}, device_id_type=MESH)

    def plane_peer(m):
        dx, dy, dc = m // 8, (m // 2) % NY, m % 2
        return {
            "blk": zi * 8 + ((yi + dy) % NY) * 2 + (ci + dc) % 2,
            "col": (xi + dx) % NX,
        }

    def greet(m, carry):
        pl.semaphore_signal(barrier, inc=1, device_id=plane_peer(m), device_id_type=MESH)
        return carry

    lax.fori_loop(1, PLANE, greet, 0)

    def raw_copies(k):
        return [
            pltpu.make_async_copy(
                ref.at[pl.ds(k * CHUNK, CHUNK)], raw.at[k % 2, i], raw_sem.at[k % 2, i]
            )
            for i, ref in enumerate((real_ref, imag_ref))
        ]

    for copy in raw_copies(0):
        copy.start()
    pick_row[...] = jnp.zeros((1, 128), jnp.int32)
    pick_row[0:1, 0:64] = picks_ref[...]

    def pick_copy(q):
        dz, dy, dc = reader(q)
        return pltpu.make_async_remote_copy(
            src_ref=pick_row,
            dst_ref=pick_in.at[q],
            send_sem=pick_send.at[q],
            recv_sem=pick_recv.at[q],
            device_id={"blk": device(-dz, -dy, dc)},
            device_id_type=MESH,
        )

    degs[0] = jnp.zeros((8, ORDER), jnp.float32)
    sums[0] = jnp.zeros((GROUP, ORDER), jnp.float32)
    ones = jnp.ones((8, ORDER), jnp.bfloat16)

    def load_chunk(k, carry):
        @pl.when(k + 1 < TILES // CHUNK)
        def _():
            for copy in raw_copies(k + 1):
                copy.start()

        for copy in raw_copies(k):
            copy.wait()

        def one(i, c):
            t = k * CHUNK + i
            row, slot = rows_ref[t], slots_ref[t]
            before_t = jnp.int32(0)
            for q in range(RB):
                last_q = last_ref[q]
                before_t = jnp.where(row == q, last_q, before_t)
                last_ref[q] = jnp.where(row == q, t + 1, last_q)
            prev_ref[t] = before_t
            owner = slot - RB
            dz = (owner // 8 - zi + NZ) % NZ
            place = jnp.where(dz < 4, 2 * dz, jnp.where(dz == 4, 7, 15 - 2 * dz))
            j = ((yi - (owner // 2) % NY + NY) % NY) * 2 + (ci + owner) % 2
            src_ref[t] = jnp.where(t < NEAR, slot, j * 8 + place)
            re_t = raw[k % 2, 0, i].T
            im_t = raw[k % 2, 1, i].T
            weights[t, 0:ORDER] = re_t
            weights[t, ORDER : 2 * ORDER] = im_t
            count = jnp.dot(ones, jnp.abs(re_t) + jnp.abs(im_t), preferred_element_type=jnp.float32)
            degs[t + 1] = count + degs[before_t]
            return c

        return lax.fori_loop(0, CHUNK, one, carry, unroll=CHUNK)

    for r in range(RB):
        last_ref[r] = jnp.int32(0)
    lax.fori_loop(0, TILES // CHUNK // 2, load_chunk, 0)
    pl.semaphore_wait(barrier, len(others) + PLANE - 1)
    for q in range(1, 32):
        pick_copy(q).start()
    lax.fori_loop(TILES // CHUNK // 2, TILES // CHUNK, load_chunk, 0)
    for r in range(RB):
        scale[r] = 1.0 / jnp.sqrt(jnp.maximum(degs[last_ref[r]], 1.0))

    pick_in[0] = pick_row[...]
    for q in range(1, 32):
        pick_copy(q).wait()
    to_smem = pltpu.make_async_copy(pick_in, pick_s, pick_loc.at[0])
    to_smem.start()
    to_smem.wait()

    to_row = lax.broadcasted_iota(jnp.int32, (GROUP, GROUP), 0)
    from_row = lax.broadcasted_iota(jnp.int32, (GROUP, GROUP), 1)
    part_first = (from_row == (to_row % HALF) * 2 + to_row // HALF).astype(jnp.float32)
    for r in range(RB):
        field[r] = jnp.dot(
            part_first,
            y_ref[:, r * ORDER : (r + 1) * ORDER],
            precision=lax.Precision.HIGHEST,
            preferred_element_type=jnp.float32,
        )

    def z_copy(par, way, kind, half):
        source = own[par] if kind == 0 else zbuf[1 + way][par]
        part = pl.ds(half * 2, 2)
        return pltpu.make_async_remote_copy(
            src_ref=source.at[part],
            dst_ref=zbuf[1 + 2 * kind + way][par].at[part],
            send_sem=z_send.at[par, way, kind, half],
            recv_sem=z_recv.at[par, way, kind, half],
            device_id={"blk": device(-1 if way else 1, 0, 0)},
            device_id_type=MESH,
        )

    def w_copy(par, q):
        dz, dy, dc = reader(q)
        return pltpu.make_async_remote_copy(
            src_ref=away[par].at[q - 8],
            dst_ref=arr[par].at[dy * 2 + dc, 5 if dz == 1 else 6 if dz == -1 else 7],
            send_sem=w_send.at[par, q - 8],
            recv_sem=w_recv.at[par, q - 8],
            device_id={"blk": device(dz, dy, dc)},
            device_id_type=MESH,
        )

    def y_copy(par, j, g):
        first, count = GROUPS[g]
        return pltpu.make_async_remote_copy(
            src_ref=stage[par].at[j, pl.ds(first, count)],
            dst_ref=arr[par].at[j, pl.ds(first, count)],
            send_sem=y_send.at[par, j, g],
            recv_sem=y_recv.at[par, j, g],
            device_id={"blk": partner(j)},
            device_id_type=MESH,
        )

    def hand_on(par, g):
        first, count = GROUPS[g]
        for j in (2, 3, 6, 7, 4, 5, 1, 0):
            if j == 0 and g == 0:
                continue
            for k in range(first, first + count):
                source = own[par] if k == 0 else zbuf[k][par]
                owner = device(Z_OFFSET[k], 0, 0)
                block = source[pick_s[j, 0, owner]]
                if j == 0:
                    arr[par][0, k] = block
                else:
                    stage[par][j, k] = block
            if j != 0:
                y_copy(par, j, g).start()

    def product(block, t):
        lower = block[HALF:GROUP]
        left = jnp.concatenate([block, jnp.concatenate([-lower, block[0:HALF]], axis=0)], axis=1)
        sums[t + 1] = sums[prev_ref[t]] + jnp.dot(
            left, weights[t], preferred_element_type=jnp.float32
        )

    before[...] = jnp.zeros_like(before)

    def apply(par, factor):
        for r in range(RB):
            s4 = jnp.concatenate([scale[r]] * 4, axis=0)
            own[par][r] = (field[r] * s4).astype(jnp.bfloat16)
        for half in range(4):
            for way in range(2):
                z_copy(par, way, 0, half).start()
        hand_on(par, 0)

        def near(t, c):
            product(own[par][src_ref[t]], t)
            return c

        lax.fori_loop(0, NEAR, near, 0, unroll=UNROLL)
        for half in range(4):
            for way in range(2):
                z_copy(par, way, 0, half).wait_recv()
                z_copy(par, way, 1, half).start()
        hand_on(par, 1)
        for half in range(4):
            for way in range(2):
                z_copy(par, way, 1, half).wait_recv()
        for first in (24, 8):
            for i in range(4 if first == 24 else 8):
                for way in range(2):
                    q = first + way * (4 if first == 24 else 8) + i
                    owner = device(2 if way else -2, 0, 0)
                    away[par][q - 8] = zbuf[3 + way][par][pick_s[q, 0, owner]]
                    w_copy(par, q).start()
        hand_on(par, 2)
        for kind in range(2):
            for way in range(2):
                for half in range(4):
                    z_copy(par, way, kind, half).wait_send()
        for g in range(3):
            for j in range(1, 8):
                y_copy(par, j, g).wait_send()
        for q in range(8, 32):
            w_copy(par, q).wait_send()
        for g in range(3):
            for j in range(1, 8):
                y_copy(par, j, g).wait_recv()
        for q in range(8, 32):
            w_copy(par, q).wait_recv()

        def far(t, c):
            place = src_ref[t]
            product(arr[par][place // 8, place % 8], t)
            return c

        lax.fori_loop(NEAR, TILES, far, 0, unroll=40)
        for r in range(RB):
            s4 = jnp.concatenate([scale[r]] * 4, axis=0)
            now = field[r]
            moved = ((1.0 - center) * now - sums[last_ref[r]] * s4) / half_width
            field[r] = factor * moved - before[r]
            before[r] = now

    def two_steps(i, c):
        apply(0, jnp.where(i == 0, 1.0, 2.0).astype(jnp.float32))
        apply(1, 2.0)
        return c

    lax.fori_loop(0, STEPS // 2, two_steps, 0)

    def x_copy(dx):
        to = (xi + dx) % NX
        return pltpu.make_async_remote_copy(
            src_ref=field.at[pl.ds(to * 2, 2)],
            dst_ref=quarter.at[xi],
            send_sem=x_send.at[dx],
            recv_sem=x_recv.at[dx],
            device_id={"col": to},
            device_id_type=MESH,
        )

    for dx in (2, 1, 3):
        x_copy(dx).start()
    quarter[xi] = field[pl.ds(xi * 2, 2)]
    for dx in range(1, NX):
        x_copy(dx).wait()
    for b in range(2):
        cols = slice(b * ORDER, (b + 1) * ORDER)
        for q in range(NX):
            joined[q * HALF : (q + 1) * HALF, cols] = quarter[q, b, 0:HALF]
            joined[VEC + q * HALF : VEC + (q + 1) * HALF, cols] = quarter[q, b, HALF:GROUP]

    gram = jnp.zeros((VEC, 2 * VEC), jnp.float32)
    for b in range(2):
        cols = slice(b * ORDER, (b + 1) * ORDER)
        top, low = joined[0:VEC, cols], joined[VEC : 2 * VEC, cols]
        right = jnp.concatenate(
            [jnp.concatenate([top, low], axis=1), jnp.concatenate([-low, top], axis=1)], axis=0
        )
        gram += lax.dot_general(
            jnp.concatenate([top, low], axis=1),
            right,
            (((1,), (1,)), ((), ())),
            precision=lax.Precision.HIGHEST,
            preferred_element_type=jnp.float32,
        )
    for i in range(8):
        pieces[i] = gram[i * 8 : (i + 1) * 8]

    def a_copy(dz):
        to = (zi + dz) % NZ
        return pltpu.make_async_remote_copy(
            src_ref=pieces.at[to],
            dst_ref=by_z.at[zi],
            send_sem=a_send.at[dz],
            recv_sem=a_recv.at[dz],
            device_id={"blk": (me + 8 * dz) % 64},
            device_id_type=MESH,
        )

    for dz in range(1, NZ):
        a_copy(dz).start()
    by_z[zi] = pieces[zi]
    for dz in range(1, NZ):
        a_copy(dz).wait()
    mine = by_z[0]
    for i in range(1, NZ):
        mine += by_z[i]
    place = xi * 8 + yi * 2 + ci
    by_plane[place] = mine

    def b_copy(m):
        return pltpu.make_async_remote_copy(
            src_ref=by_plane.at[place],
            dst_ref=by_plane.at[place],
            send_sem=b_send.at[m],
            recv_sem=b_recv.at[m],
            device_id=plane_peer(m),
            device_id_type=MESH,
        )

    def b_start(m, carry):
        b_copy(m).start()
        return carry

    def b_wait(m, carry):
        b_copy(m).wait()
        return carry

    lax.fori_loop(1, PLANE, b_start, 0, unroll=31)
    lax.fori_loop(1, PLANE, b_wait, 0, unroll=31)
    mine = by_plane[0]
    for i in range(1, PLANE):
        mine += by_plane[i]
    total[zi] = mine

    def c_copy(dz):
        return pltpu.make_async_remote_copy(
            src_ref=total.at[zi],
            dst_ref=total.at[zi],
            send_sem=c_send.at[dz],
            recv_sem=c_recv.at[dz],
            device_id={"blk": (me + 8 * dz) % 64},
            device_id_type=MESH,
        )

    for dz in range(1, NZ):
        c_copy(dz).start()
    for dz in range(1, NZ):
        c_copy(dz).wait()

    wide = (VEC, 2 * VEC)
    sub = lax.broadcasted_iota(jnp.int32, wide, 0)
    lane = lax.broadcasted_iota(jnp.int32, wide, 1)
    sign = jnp.where(lane < VEC, -1.0, 1.0).astype(jnp.float32)
    for i in range(8):
        elim[i * 8 : (i + 1) * 8] = total[i]
    inverse[...] = (lane == sub).astype(jnp.float32)

    def eliminate(k, carry):
        a, v = elim[...], inverse[...]
        a_row = jnp.broadcast_to(elim[pl.ds(k, 1)], wide)
        v_row = jnp.broadcast_to(inverse[pl.ds(k, 1)], wide)
        pivot = jnp.sum(jnp.where(lane == k, a_row, 0.0), axis=1, keepdims=True)
        col_re = jnp.sum(jnp.where(lane == k, a, 0.0), axis=1, keepdims=True)
        col_im = jnp.sum(jnp.where(lane == k + VEC, a, 0.0), axis=1, keepdims=True)
        below = sub > k
        m_re = jnp.where(below, col_re / pivot, 0.0)
        m_im = jnp.where(below, col_im / pivot, 0.0)
        a_turned = pltpu.roll(a_row, VEC, 1) * sign
        v_turned = pltpu.roll(v_row, VEC, 1) * sign
        elim[...] = a - m_re * a_row - m_im * a_turned
        inverse[...] = v - m_re * v_row - m_im * v_turned
        return carry

    lax.fori_loop(0, VEC, eliminate, 0)
    pivots = jnp.sum(jnp.where(lane == sub, elim[...], 0.0), axis=1, keepdims=True)
    scaled = inverse[...] * (math.sqrt(NODES) / jnp.sqrt(pivots))
    solver[pl.ds(0, VEC, stride=2), :] = -sign * scaled
    solver[pl.ds(1, VEC, stride=2), :] = pltpu.roll(scaled, VEC, 1)

    def e_copy(dx):
        to = (xi + dx) % NX
        return pltpu.make_async_remote_copy(
            src_ref=solved.at[to],
            dst_ref=landed.at[xi],
            send_sem=e_send.at[dx],
            recv_sem=e_recv.at[dx],
            device_id={"col": to},
            device_id_type=MESH,
        )

    for dx in (2, 1, 3, 0):
        to = (xi + dx) % NX
        part = jnp.dot(
            solver[pl.ds(to * GROUP, GROUP)],
            joined[...],
            precision=lax.Precision.HIGHEST,
            preferred_element_type=jnp.float32,
        )
        if dx:
            solved[to] = part
            e_copy(dx).start()
        else:
            landed[xi] = part
    for dx in range(1, NX):
        e_copy(dx).wait()
    for q in range(NX):
        out_ref[:, q * 512 : (q + 1) * 512] = landed[q]


def per_device(y_start, tile_real, tile_imag, tile_rows, tile_slots, fetch_pick):
    block = (RB, GROUP, ORDER)
    tiny = (8, 8, 128)
    dma = pltpu.SemaphoreType.DMA
    return pl.pallas_call(
        filter_kernel,
        name="filter",
        out_shape=jax.ShapeDtypeStruct(y_start.shape, jnp.float32),
        in_specs=[pl.BlockSpec(memory_space=pltpu.SMEM)] * 2
        + [pl.BlockSpec(memory_space=pltpu.VMEM)] * 2
        + [pl.BlockSpec(memory_space=pl.ANY)] * 2,
        out_specs=pl.BlockSpec(memory_space=pltpu.VMEM),
        scratch_shapes=[pltpu.VMEM(block, jnp.bfloat16)] * 10
        + [pltpu.VMEM((8,) + block, jnp.bfloat16)] * 4
        + [pltpu.VMEM((24,) + block[1:], jnp.bfloat16)] * 2
        + [
            pltpu.VMEM((TILES, 2 * ORDER, ORDER), jnp.bfloat16),
            pltpu.VMEM((2, 2, CHUNK, ORDER, ORDER), jnp.bfloat16),
            pltpu.VMEM((TILES + 1, GROUP, ORDER), jnp.float32),
            pltpu.VMEM((TILES + 1, 8, ORDER), jnp.float32),
            pltpu.VMEM((RB, 8, ORDER), jnp.float32),
            pltpu.VMEM(block, jnp.float32),
            pltpu.VMEM(block, jnp.float32),
            pltpu.VMEM((32, 1, 128), jnp.int32),
            pltpu.SMEM((32, 1, 128), jnp.int32),
            pltpu.SMEM((TILES,), jnp.int32),
            pltpu.SMEM((RB,), jnp.int32),
            pltpu.SMEM((TILES,), jnp.int32),
            pltpu.VMEM((NX, 2, GROUP, ORDER), jnp.float32),
            pltpu.VMEM((2 * VEC, 512), jnp.float32),
            pltpu.VMEM(tiny, jnp.float32),
            pltpu.VMEM(tiny, jnp.float32),
            pltpu.VMEM((PLANE, 8, 128), jnp.float32),
            pltpu.VMEM(tiny, jnp.float32),
            pltpu.VMEM((VEC, 2 * VEC), jnp.float32),
            pltpu.VMEM((VEC, 2 * VEC), jnp.float32),
            pltpu.VMEM((2 * VEC, 2 * VEC), jnp.float32),
            pltpu.VMEM((NX, GROUP, 512), jnp.float32),
            pltpu.VMEM((NX, GROUP, 512), jnp.float32),
            pltpu.VMEM((1, 128), jnp.int32),
            dma((2, 2)),
            dma((32,)),
            dma((32,)),
            dma((1,)),
            dma((2, 2, 2, 4)),
            dma((2, 2, 2, 4)),
            dma((2, 8, 3)),
            dma((2, 8, 3)),
            dma((2, 24)),
            dma((2, 24)),
            dma((NX,)),
            dma((NX,)),
            dma((NZ,)),
            dma((NZ,)),
            dma((PLANE,)),
            dma((PLANE,)),
            dma((NZ,)),
            dma((NZ,)),
            dma((NX,)),
            dma((NX,)),
        ],
        compiler_params=pltpu.CompilerParams(
            collective_id=0, has_side_effects=True, vmem_limit_bytes=60 << 20
        ),
    )(tile_rows, tile_slots, y_start, fetch_pick, tile_real, tile_imag)


def solution(mesh):
    return jax.shard_map(
        per_device,
        mesh=mesh,
        in_specs=(
            P("col", "blk"),
            P("blk", None, None),
            P("blk", None, None),
            P("blk"),
            P("blk"),
            P("blk", None),
        ),
        out_specs=P("col", "blk"),
        check_vma=False,
    )
```

```python
import math

import jax
import jax.numpy as jnp
from jax import lax
from jax.experimental import pallas as pl
from jax.experimental.pallas import tpu as pltpu
from jax.sharding import PartitionSpec as P

STEPS = 4
NEAR = 16
TILES = 96
RB = 8
GROUP = 32
HALF = 16
ORDER = 256
NZ, NY, NX = 8, 4, 4
PLANE = 32
VEC = 64
NODES = 131072
CHUNK = 8
UNROLL = 16
MESH = pl.DeviceIdType.MESH

center = 1.25
half_width = 0.75

Z_PLACE = (0, 2, 4, 6, 7, 5, 3, 1)
Z_OFFSET = (0, 7, 1, 6, 2, 5, 3, 4)
GROUPS = ((0, 1), (1, 2), (3, 2))


def filter_kernel(rows_ref, slots_ref, y_ref, picks_ref, real_ref, imag_ref, out_ref, *scratch):
    own = scratch[0:2]
    zbuf = (None,) + tuple(scratch[2 + 2 * i : 4 + 2 * i] for i in range(4))
    arr = scratch[10:12]
    stage = scratch[12:14]
    away = scratch[14:16]
    (
        weights, raw, sums, degs, scale, field, before,
        pick_in, pick_s, prev_ref, last_ref, src_ref,
        quarter, joined, pieces, by_z, by_plane, total, elim, inverse, solver, solved, landed, pick_row,
        raw_sem, pick_send, pick_recv, pick_loc, z_send, z_recv, y_send, y_recv, w_send, w_recv,
        x_send, x_recv, a_send, a_recv, b_send, b_recv, c_send, c_recv, e_send, e_recv,
    ) = scratch[16:]
    xi = lax.axis_index("col")
    me = lax.axis_index("blk")
    zi, yi, ci = me // 8, (me // 2) % NY, me % 2
    ids = {
        (dz, dy, dc): ((zi + dz) % NZ) * 8 + ((yi + dy) % NY) * 2 + (ci + dc) % 2
        for dz in range(NZ)
        for dy in range(NY)
        for dc in range(2)
    }

    def device(dz, dy, dc):
        return ids[dz % NZ, dy % NY, dc % 2]

    def partner(j):
        return device(0, j // 2, j % 2)

    def reader(q):
        if q < 8:
            return 0, q // 2, q % 2
        if q < 24:
            return (1 if q < 16 else -1), (q % 8) // 2, q % 2
        return (2, q - 24, 0) if q < 28 else (-2, q - 28, 1)

    barrier = pltpu.get_barrier_semaphore()
    others = [(dz, j // 2, j % 2) for dz in (1, -1, 2, -2) for j in range(8)]
    others += [(dz, 0, 0) for dz in (3, 4, -3)]
    for other in others:
        pl.semaphore_signal(barrier, inc=1, device_id={"blk": device(*other)}, device_id_type=MESH)

    def plane_peer(m):
        dx, dy, dc = m // 8, (m // 2) % NY, m % 2
        return {
            "blk": zi * 8 + ((yi + dy) % NY) * 2 + (ci + dc) % 2,
            "col": (xi + dx) % NX,
        }

    def greet(m, carry):
        pl.semaphore_signal(barrier, inc=1, device_id=plane_peer(m), device_id_type=MESH)
        return carry

    lax.fori_loop(1, PLANE, greet, 0)

    def raw_copies(k):
        return [
            pltpu.make_async_copy(
                ref.at[pl.ds(k * CHUNK, CHUNK)], raw.at[k % 2, i], raw_sem.at[k % 2, i]
            )
            for i, ref in enumerate((real_ref, imag_ref))
        ]

    for copy in raw_copies(0):
        copy.start()
    pick_row[...] = jnp.zeros((1, 128), jnp.int32)
    pick_row[0:1, 0:64] = picks_ref[...]

    def pick_copy(q):
        dz, dy, dc = reader(q)
        return pltpu.make_async_remote_copy(
            src_ref=pick_row,
            dst_ref=pick_in.at[q],
            send_sem=pick_send.at[q],
            recv_sem=pick_recv.at[q],
            device_id={"blk": device(-dz, -dy, dc)},
            device_id_type=MESH,
        )

    degs[0] = jnp.zeros((8, ORDER), jnp.float32)
    sums[0] = jnp.zeros((GROUP, ORDER), jnp.float32)
    ones = jnp.ones((8, ORDER), jnp.bfloat16)

    def load_chunk(k, carry):
        @pl.when(k + 1 < TILES // CHUNK)
        def _():
            for copy in raw_copies(k + 1):
                copy.start()

        for copy in raw_copies(k):
            copy.wait()

        def one(i, c):
            t = k * CHUNK + i
            row, slot = rows_ref[t], slots_ref[t]
            before_t = jnp.int32(0)
            for q in range(RB):
                last_q = last_ref[q]
                before_t = jnp.where(row == q, last_q, before_t)
                last_ref[q] = jnp.where(row == q, t + 1, last_q)
            prev_ref[t] = before_t
            owner = slot - RB
            dz = (owner // 8 - zi + NZ) % NZ
            place = jnp.where(dz < 4, 2 * dz, jnp.where(dz == 4, 7, 15 - 2 * dz))
            j = ((yi - (owner // 2) % NY + NY) % NY) * 2 + (ci + owner) % 2
            src_ref[t] = jnp.where(t < NEAR, slot, j * 8 + place)
            re_t = raw[k % 2, 0, i].T
            im_t = raw[k % 2, 1, i].T
            weights[t, 0:ORDER] = re_t
            weights[t, ORDER : 2 * ORDER] = im_t
            count = jnp.dot(ones, jnp.abs(re_t) + jnp.abs(im_t), preferred_element_type=jnp.float32)
            degs[t + 1] = count + degs[before_t]
            return c

        return lax.fori_loop(0, CHUNK, one, carry, unroll=CHUNK)

    for r in range(RB):
        last_ref[r] = jnp.int32(0)
    lax.fori_loop(0, TILES // CHUNK // 2, load_chunk, 0)
    pl.semaphore_wait(barrier, len(others) + PLANE - 1)
    for q in range(1, 32):
        pick_copy(q).start()
    lax.fori_loop(TILES // CHUNK // 2, TILES // CHUNK, load_chunk, 0)
    for r in range(RB):
        scale[r] = 1.0 / jnp.sqrt(jnp.maximum(degs[last_ref[r]], 1.0))

    pick_in[0] = pick_row[...]
    for q in range(1, 32):
        pick_copy(q).wait()
    to_smem = pltpu.make_async_copy(pick_in, pick_s, pick_loc.at[0])
    to_smem.start()
    to_smem.wait()

    to_row = lax.broadcasted_iota(jnp.int32, (GROUP, GROUP), 0)
    from_row = lax.broadcasted_iota(jnp.int32, (GROUP, GROUP), 1)
    part_first = (from_row == (to_row % HALF) * 2 + to_row // HALF).astype(jnp.float32)
    for r in range(RB):
        field[r] = jnp.dot(
            part_first,
            y_ref[:, r * ORDER : (r + 1) * ORDER],
            precision=lax.Precision.HIGHEST,
            preferred_element_type=jnp.float32,
        )

    def z_copy(par, way, kind, half):
        source = own[par] if kind == 0 else zbuf[1 + way][par]
        part = pl.ds(half * 2, 2)
        return pltpu.make_async_remote_copy(
            src_ref=source.at[part],
            dst_ref=zbuf[1 + 2 * kind + way][par].at[part],
            send_sem=z_send.at[par, way, kind, half],
            recv_sem=z_recv.at[par, way, kind, half],
            device_id={"blk": device(-1 if way else 1, 0, 0)},
            device_id_type=MESH,
        )

    def w_copy(par, q):
        dz, dy, dc = reader(q)
        return pltpu.make_async_remote_copy(
            src_ref=away[par].at[q - 8],
            dst_ref=arr[par].at[dy * 2 + dc, 5 if dz == 1 else 6 if dz == -1 else 7],
            send_sem=w_send.at[par, q - 8],
            recv_sem=w_recv.at[par, q - 8],
            device_id={"blk": device(dz, dy, dc)},
            device_id_type=MESH,
        )

    def y_copy(par, j, g):
        first, count = GROUPS[g]
        return pltpu.make_async_remote_copy(
            src_ref=stage[par].at[j, pl.ds(first, count)],
            dst_ref=arr[par].at[j, pl.ds(first, count)],
            send_sem=y_send.at[par, j, g],
            recv_sem=y_recv.at[par, j, g],
            device_id={"blk": partner(j)},
            device_id_type=MESH,
        )

    def hand_on(par, g):
        first, count = GROUPS[g]
        for j in (2, 3, 6, 7, 4, 5, 1, 0):
            if j == 0 and g == 0:
                continue
            for k in range(first, first + count):
                source = own[par] if k == 0 else zbuf[k][par]
                owner = device(Z_OFFSET[k], 0, 0)
                block = source[pick_s[j, 0, owner]]
                if j == 0:
                    arr[par][0, k] = block
                else:
                    stage[par][j, k] = block
            if j != 0:
                y_copy(par, j, g).start()

    def product(block, t):
        lower = block[HALF:GROUP]
        left = jnp.concatenate([block, jnp.concatenate([-lower, block[0:HALF]], axis=0)], axis=1)
        sums[t + 1] = sums[prev_ref[t]] + jnp.dot(
            left, weights[t], preferred_element_type=jnp.float32
        )

    before[...] = jnp.zeros_like(before)

    def apply(par, factor):
        for r in range(RB):
            s4 = jnp.concatenate([scale[r]] * 4, axis=0)
            own[par][r] = (field[r] * s4).astype(jnp.bfloat16)
        for half in range(4):
            for way in range(2):
                z_copy(par, way, 0, half).start()
        hand_on(par, 0)

        def near(t, c):
            product(own[par][src_ref[t]], t)
            return c

        lax.fori_loop(0, NEAR, near, 0, unroll=UNROLL)
        for half in range(4):
            for way in range(2):
                z_copy(par, way, 0, half).wait_recv()
                z_copy(par, way, 1, half).start()
        hand_on(par, 1)
        for half in range(4):
            for way in range(2):
                z_copy(par, way, 1, half).wait_recv()
        for first in (24, 8):
            for i in range(4 if first == 24 else 8):
                for way in range(2):
                    q = first + way * (4 if first == 24 else 8) + i
                    owner = device(2 if way else -2, 0, 0)
                    away[par][q - 8] = zbuf[3 + way][par][pick_s[q, 0, owner]]
                    w_copy(par, q).start()
        hand_on(par, 2)
        for kind in range(2):
            for way in range(2):
                for half in range(4):
                    z_copy(par, way, kind, half).wait_send()
        for g in range(3):
            for j in range(1, 8):
                y_copy(par, j, g).wait_send()
        for q in range(8, 32):
            w_copy(par, q).wait_send()
        for g in range(3):
            for j in range(1, 8):
                y_copy(par, j, g).wait_recv()
        for q in range(8, 32):
            w_copy(par, q).wait_recv()

        def far(t, c):
            place = src_ref[t]
            product(arr[par][place // 8, place % 8], t)
            return c

        lax.fori_loop(NEAR, TILES, far, 0, unroll=40)
        for r in range(RB):
            s4 = jnp.concatenate([scale[r]] * 4, axis=0)
            now = field[r]
            moved = ((1.0 - center) * now - sums[last_ref[r]] * s4) / half_width
            field[r] = factor * moved - before[r]
            before[r] = now

    def two_steps(i, c):
        apply(0, jnp.where(i == 0, 1.0, 2.0).astype(jnp.float32))
        apply(1, 2.0)
        return c

    lax.fori_loop(0, STEPS // 2, two_steps, 0)

    def x_copy(dx):
        to = (xi + dx) % NX
        return pltpu.make_async_remote_copy(
            src_ref=field.at[pl.ds(to * 2, 2)],
            dst_ref=quarter.at[xi],
            send_sem=x_send.at[dx],
            recv_sem=x_recv.at[dx],
            device_id={"col": to},
            device_id_type=MESH,
        )

    for dx in (2, 1, 3):
        x_copy(dx).start()
    quarter[xi] = field[pl.ds(xi * 2, 2)]
    for dx in range(1, NX):
        x_copy(dx).wait()
    for b in range(2):
        cols = slice(b * ORDER, (b + 1) * ORDER)
        for q in range(NX):
            joined[q * HALF : (q + 1) * HALF, cols] = quarter[q, b, 0:HALF]
            joined[VEC + q * HALF : VEC + (q + 1) * HALF, cols] = quarter[q, b, HALF:GROUP]

    gram = jnp.zeros((VEC, 2 * VEC), jnp.float32)
    for b in range(2):
        cols = slice(b * ORDER, (b + 1) * ORDER)
        top, low = joined[0:VEC, cols], joined[VEC : 2 * VEC, cols]
        right = jnp.concatenate(
            [jnp.concatenate([top, low], axis=1), jnp.concatenate([-low, top], axis=1)], axis=0
        )
        gram += lax.dot_general(
            jnp.concatenate([top, low], axis=1),
            right,
            (((1,), (1,)), ((), ())),
            precision=lax.Precision.HIGHEST,
            preferred_element_type=jnp.float32,
        )
    for i in range(8):
        pieces[i] = gram[i * 8 : (i + 1) * 8]

    def a_copy(dz):
        to = (zi + dz) % NZ
        return pltpu.make_async_remote_copy(
            src_ref=pieces.at[to],
            dst_ref=by_z.at[zi],
            send_sem=a_send.at[dz],
            recv_sem=a_recv.at[dz],
            device_id={"blk": (me + 8 * dz) % 64},
            device_id_type=MESH,
        )

    for dz in range(1, NZ):
        a_copy(dz).start()
    by_z[zi] = pieces[zi]
    for dz in range(1, NZ):
        a_copy(dz).wait()
    mine = by_z[0]
    for i in range(1, NZ):
        mine += by_z[i]
    place = xi * 8 + yi * 2 + ci
    by_plane[place] = mine

    def b_copy(m):
        return pltpu.make_async_remote_copy(
            src_ref=by_plane.at[place],
            dst_ref=by_plane.at[place],
            send_sem=b_send.at[m],
            recv_sem=b_recv.at[m],
            device_id=plane_peer(m),
            device_id_type=MESH,
        )

    def b_start(m, carry):
        b_copy(m).start()
        return carry

    def b_wait(m, carry):
        b_copy(m).wait()
        return carry

    lax.fori_loop(1, PLANE, b_start, 0, unroll=31)
    lax.fori_loop(1, PLANE, b_wait, 0, unroll=31)
    mine = by_plane[0]
    for i in range(1, PLANE):
        mine += by_plane[i]
    total[zi] = mine

    def c_copy(dz):
        return pltpu.make_async_remote_copy(
            src_ref=total.at[zi],
            dst_ref=total.at[zi],
            send_sem=c_send.at[dz],
            recv_sem=c_recv.at[dz],
            device_id={"blk": (me + 8 * dz) % 64},
            device_id_type=MESH,
        )

    for dz in range(1, NZ):
        c_copy(dz).start()
    for dz in range(1, NZ):
        c_copy(dz).wait()

    wide = (VEC, 2 * VEC)
    sub = lax.broadcasted_iota(jnp.int32, wide, 0)
    lane = lax.broadcasted_iota(jnp.int32, wide, 1)
    sign = jnp.where(lane < VEC, -1.0, 1.0).astype(jnp.float32)
    for i in range(8):
        elim[i * 8 : (i + 1) * 8] = total[i]
    inverse[...] = (lane == sub).astype(jnp.float32)

    lane_row, sign_row = lane[0:1], sign[0:1]

    def entry(row, index):
        return jnp.sum(jnp.where(lane_row == index, row, 0.0), axis=1, keepdims=True)

    def column(matrix, index):
        return jnp.sum(jnp.where(lane == index, matrix, 0.0), axis=1, keepdims=True)

    def times_i(row):
        return pltpu.roll(row, VEC, 1) * sign_row

    def eliminate(i, carry):
        k = 2 * i
        a, v = elim[...], inverse[...]
        a0, a1 = elim[pl.ds(k, 1)], elim[pl.ds(k + 1, 1)]
        v0, v1 = inverse[pl.ds(k, 1)], inverse[pl.ds(k + 1, 1)]
        inv0 = 1.0 / entry(a0, k)
        g_re, g_im = entry(a1, k) * inv0, entry(a1, k + VEC) * inv0
        e_re, e_im = entry(a0, k + 1), entry(a0, k + 1 + VEC)
        inv1 = 1.0 / (entry(a1, k + 1) - (g_re * e_re - g_im * e_im))
        a0_i, v0_i = times_i(a0), times_i(v0)
        a1 = a1 - g_re * a0 - g_im * a0_i
        v1 = v1 - g_re * v0 - g_im * v0_i
        a1_i, v1_i = times_i(a1), times_i(v1)
        m0_re = jnp.where(sub > k, column(a, k) * inv0, 0.0)
        m0_im = jnp.where(sub > k, column(a, k + VEC) * inv0, 0.0)
        c_re = column(a, k + 1) - (m0_re * e_re - m0_im * e_im)
        c_im = column(a, k + 1 + VEC) - (m0_re * e_im + m0_im * e_re)
        m1_re = jnp.where(sub > k + 1, c_re * inv1, 0.0)
        m1_im = jnp.where(sub > k + 1, c_im * inv1, 0.0)
        elim[...] = a - m0_re * a0 - m0_im * a0_i - m1_re * a1 - m1_im * a1_i
        inverse[...] = v - m0_re * v0 - m0_im * v0_i - m1_re * v1 - m1_im * v1_i
        return carry

    lax.fori_loop(0, VEC // 2, eliminate, 0)
    pivots = jnp.sum(jnp.where(lane == sub, elim[...], 0.0), axis=1, keepdims=True)
    scaled = inverse[...] * (math.sqrt(NODES) / jnp.sqrt(pivots))
    solver[pl.ds(0, VEC, stride=2), :] = -sign * scaled
    solver[pl.ds(1, VEC, stride=2), :] = pltpu.roll(scaled, VEC, 1)

    def e_copy(dx):
        to = (xi + dx) % NX
        return pltpu.make_async_remote_copy(
            src_ref=solved.at[to],
            dst_ref=landed.at[xi],
            send_sem=e_send.at[dx],
            recv_sem=e_recv.at[dx],
            device_id={"col": to},
            device_id_type=MESH,
        )

    for dx in (2, 1, 3, 0):
        to = (xi + dx) % NX
        part = jnp.dot(
            solver[pl.ds(to * GROUP, GROUP)],
            joined[...],
            precision=lax.Precision.HIGHEST,
            preferred_element_type=jnp.float32,
        )
        if dx:
            solved[to] = part
            e_copy(dx).start()
        else:
            landed[xi] = part
    for dx in range(1, NX):
        e_copy(dx).wait()
    for q in range(NX):
        out_ref[:, q * 512 : (q + 1) * 512] = landed[q]


def per_device(y_start, tile_real, tile_imag, tile_rows, tile_slots, fetch_pick):
    block = (RB, GROUP, ORDER)
    tiny = (8, 8, 128)
    dma = pltpu.SemaphoreType.DMA
    return pl.pallas_call(
        filter_kernel,
        name="filter",
        out_shape=jax.ShapeDtypeStruct(y_start.shape, jnp.float32),
        in_specs=[pl.BlockSpec(memory_space=pltpu.SMEM)] * 2
        + [pl.BlockSpec(memory_space=pltpu.VMEM)] * 2
        + [pl.BlockSpec(memory_space=pl.ANY)] * 2,
        out_specs=pl.BlockSpec(memory_space=pltpu.VMEM),
        scratch_shapes=[pltpu.VMEM(block, jnp.bfloat16)] * 10
        + [pltpu.VMEM((8,) + block, jnp.bfloat16)] * 4
        + [pltpu.VMEM((24,) + block[1:], jnp.bfloat16)] * 2
        + [
            pltpu.VMEM((TILES, 2 * ORDER, ORDER), jnp.bfloat16),
            pltpu.VMEM((2, 2, CHUNK, ORDER, ORDER), jnp.bfloat16),
            pltpu.VMEM((TILES + 1, GROUP, ORDER), jnp.float32),
            pltpu.VMEM((TILES + 1, 8, ORDER), jnp.float32),
            pltpu.VMEM((RB, 8, ORDER), jnp.float32),
            pltpu.VMEM(block, jnp.float32),
            pltpu.VMEM(block, jnp.float32),
            pltpu.VMEM((32, 1, 128), jnp.int32),
            pltpu.SMEM((32, 1, 128), jnp.int32),
            pltpu.SMEM((TILES,), jnp.int32),
            pltpu.SMEM((RB,), jnp.int32),
            pltpu.SMEM((TILES,), jnp.int32),
            pltpu.VMEM((NX, 2, GROUP, ORDER), jnp.float32),
            pltpu.VMEM((2 * VEC, 512), jnp.float32),
            pltpu.VMEM(tiny, jnp.float32),
            pltpu.VMEM(tiny, jnp.float32),
            pltpu.VMEM((PLANE, 8, 128), jnp.float32),
            pltpu.VMEM(tiny, jnp.float32),
            pltpu.VMEM((VEC, 2 * VEC), jnp.float32),
            pltpu.VMEM((VEC, 2 * VEC), jnp.float32),
            pltpu.VMEM((2 * VEC, 2 * VEC), jnp.float32),
            pltpu.VMEM((NX, GROUP, 512), jnp.float32),
            pltpu.VMEM((NX, GROUP, 512), jnp.float32),
            pltpu.VMEM((1, 128), jnp.int32),
            dma((2, 2)),
            dma((32,)),
            dma((32,)),
            dma((1,)),
            dma((2, 2, 2, 4)),
            dma((2, 2, 2, 4)),
            dma((2, 8, 3)),
            dma((2, 8, 3)),
            dma((2, 24)),
            dma((2, 24)),
            dma((NX,)),
            dma((NX,)),
            dma((NZ,)),
            dma((NZ,)),
            dma((PLANE,)),
            dma((PLANE,)),
            dma((NZ,)),
            dma((NZ,)),
            dma((NX,)),
            dma((NX,)),
        ],
        compiler_params=pltpu.CompilerParams(
            collective_id=0, has_side_effects=True, vmem_limit_bytes=60 << 20
        ),
    )(tile_rows, tile_slots, y_start, fetch_pick, tile_real, tile_imag)


def solution(mesh):
    return jax.shard_map(
        per_device,
        mesh=mesh,
        in_specs=(
            P("col", "blk"),
            P("blk", None, None),
            P("blk", None, None),
            P("blk"),
            P("blk"),
            P("blk", None),
        ),
        out_specs=P("col", "blk"),
        check_vma=False,
    )
```
